512 devices in a mesh: grp: 16 (over y_lo, z), tp: 8 (over x, core), sp: 4 (over y_hi).
Axes of the slice: x: 4, y: 8 (y_hi: 4, y_lo: 2; y = y_hi * 2 + y_lo), z: 8, core: 2. Of those that a mesh axis runs over, the one named last changes fastest.
Arguments:
- queries: bfloat16 [10240, 8192], P(('grp', 'sp'), 'tp'), may hold values from -6 to 6
- rotated_key_rows: bfloat16 [10240, 1024], P(('grp', 'sp'), 'tp'), may hold values from -6 to 6
- values: bfloat16 [10240, 1024], P(('grp', 'sp'), 'tp'), may hold values from -12 to 12
- packed_prompt_length: int32 [16, 3], P('grp'), may hold values from 1 to 320, 640 in all within a row
- output_projection_weight: bfloat16 [8192, 8192], P('tp', 'sp'), may hold values from -0.0625 to 0.0625
- adapter_down_maps: bfloat16 [64, 64, 8192], P('grp', None, ('tp', 'sp')), may hold values from -0.0625 to 0.0625
- adapter_up_maps: bfloat16 [64, 64, 8192], P('grp', None, ('sp', 'tp')), may hold values from -0.75 to 0.75
- tenant_adapter_slot: int32 [64], replicated, may hold values from 0 to 63, as said below
- tenant_per_block: int32 [16, 5], replicated, may hold values from 0 to 63, as said below
Outputs:
- adapted_layer_output: bfloat16 [10240, 8192], P(('grp', 'tp'), 'sp')
The draws below stay inside these ranges and needn't reach their ends.
Inputs may be any that keep to these rules, and one draw needn't show every extreme that they name: A permutation: tenant a's adapter is row tenant_adapter_slot[a] of adapter_down_maps and adapter_up_maps, held by grp index tenant_adapter_slot[a] // 4. `tenant_per_block`: the blocks of one group name distinct tenants; at most 1 of a group's tenants have slots held by one grp index, and in every group some grp index holds exactly 1 of them.
All inputs are finite; a program needn't handle non-finite values.
Results may differ from the reference program's by a relative error of at most 0.024.
Values may be sent and summed in bfloat16 or wider, within the bound.
A program may use at most 64 MiB of HBM per device.

```python
import math
import jax
import jax.numpy as jnp
import numpy as np
from jax import lax

MODEL_WIDTH = 8192
HQ = 64
KVH = 8
HS = 128
ADAPTER_RANK = 64
BLOCK = 128
PROMPTS = 3
SLOTS = 4
GROUPS = 16
TOKENS = 640
OUTPUT_FEATURES = 8192
BLOCKS = 5
ADAPTER_TOTAL = 64
CAP = 1
N_TP = 8


def draw_queries(key, part):
    key = jax.random.fold_in(key, 11)
    drawn = jax.random.normal(key, (GROUPS * TOKENS, OUTPUT_FEATURES), jnp.float32)
    drawn = jnp.clip(drawn, -6.0, 6.0)
    return drawn.astype(jnp.bfloat16)


def draw_rotated_key_rows(key, part):
    key = jax.random.fold_in(key, 23)
    drawn = jax.random.normal(key, (GROUPS * TOKENS, KVH * HS), jnp.float32)
    drawn = jnp.clip(drawn, -6.0, 6.0)
    return drawn.astype(jnp.bfloat16)


def routing_tables(key):
    slot_perm = jax.random.permutation(jax.random.fold_in(key, 5), ADAPTER_TOTAL).astype(jnp.int32)
    inverse = jnp.zeros((ADAPTER_TOTAL,), jnp.int32).at[slot_perm].set(jnp.arange(ADAPTER_TOTAL, dtype=jnp.int32))
    tenant_key = jax.random.fold_in(key, 6)

    def one_group(group_key):
        owner_order = jax.random.permutation(jax.random.fold_in(group_key, 1), GROUPS * CAP)[:BLOCKS].astype(jnp.int32)
        owner_ids = owner_order // CAP
        copy_index = owner_order % CAP
        offsets = jax.random.randint(jax.random.fold_in(group_key, 2), (GROUPS,), 0, SLOTS, jnp.int32)
        local_slot = (offsets[owner_ids] + copy_index) % SLOTS
        return inverse[owner_ids * SLOTS + local_slot]
    group_keys = jax.vmap(lambda group_id: jax.random.fold_in(tenant_key, group_id))(jnp.arange(GROUPS))
    tenants = jax.vmap(one_group)(group_keys)
    return (slot_perm, tenants.astype(jnp.int32))


def draw_tenant_adapter_slot(key, part):
    slot_perm, tenants = routing_tables(key)
    return slot_perm


def draw_tenant_per_block(key, part):
    slot_perm, tenants = routing_tables(key)
    return tenants


def block_scale(rng, shape, cuts, least, top_value):
    def one(dim, blocks):
        heights = jax.random.uniform(jax.random.fold_in(jax.random.fold_in(rng, 6), dim), (blocks,), jnp.float32, least / len(cuts), top_value / len(cuts))
        return jnp.repeat(jnp.exp(heights), shape[dim] // blocks).reshape((-1,) + (1,) * (len(shape) - dim - 1))

    loudness = one(*cuts[0])
    for cut in cuts[1:]:
        loudness = loudness * one(*cut)
    return loudness


def profile(number_of, total, limit, slope):
    portions = [(1 << 20) // math.isqrt(grade ** slope) + 1 for grade in range(2, number_of + 1)]
    spare, counts = total - limit - (number_of - 1), [1] * (number_of - 1)
    while spare > 0:
        movable = [i for i in range(number_of - 1) if counts[i] < limit]
        pool, budget = sum([portions[i] for i in movable]), spare
        for i in movable:
            more = min(limit - counts[i], max(1, budget * portions[i] // pool), spare)
            counts[i] = counts[i] + more
            spare = spare - more
    return np.array([limit] + counts)


def ragged(key, count, total, limit, lean):
    if count == 2:
        one = jax.random.randint(key, (), max(1, total - limit), min(limit, total - 1) + 1)
        return jnp.stack([one, total - one])
    sizes = jnp.asarray(profile(count, total, limit, lean), jnp.int32)
    couples = (count - 1) // 2
    source_of, receiver = sizes[1:1 + 2 * couples:2], sizes[2:2 + 2 * couples:2]
    room = jnp.minimum(source_of - 1, limit - receiver)
    moved = jax.random.randint(jax.random.fold_in(key, 1), (couples,), 0, 1 << 20) % (room + 1)
    sizes = sizes.at[1:1 + 2 * couples:2].set(source_of - moved).at[2:2 + 2 * couples:2].set(receiver + moved)
    return sizes[jax.random.permutation(jax.random.fold_in(key, 2), count)]


def scatter_about(own_key, dims, scale, reach, cuts=(), held_as=jnp.bfloat16):
    values = scale * jax.random.normal(own_key, dims, jnp.float32)
    if cuts:
        values = values * block_scale(own_key, dims, cuts, -0.22, 0.18)
    return jnp.clip(values, -reach, reach).astype(held_as)


def setup_inputs(seed: int = 0) -> dict:
    key_of = jax.random.split(jax.random.key(seed), 10)
    return {
        "queries": draw_queries(jax.random.fold_in(key_of[9], 71), 0),
        "rotated_key_rows": draw_rotated_key_rows(jax.random.fold_in(key_of[9], 71), 0),
        "values": scatter_about(key_of[2], (GROUPS * TOKENS, KVH * HS), 2.0, 12.0, ((0, 64), (1, 8))),
        "packed_prompt_length": jax.vmap(lambda own: ragged(own, PROMPTS, TOKENS, TOKENS // 2, 2))(jax.random.split(key_of[3], GROUPS)).reshape((GROUPS, PROMPTS)).astype(jnp.int32),
        "output_projection_weight": scatter_about(key_of[4], (OUTPUT_FEATURES, MODEL_WIDTH), OUTPUT_FEATURES ** -0.5, 0.0625, ((0, 8), (1, 4))),
        "adapter_down_maps": scatter_about(key_of[5], (ADAPTER_TOTAL, ADAPTER_RANK, OUTPUT_FEATURES), OUTPUT_FEATURES ** -0.5, 0.0625, ((0, 16), (2, 32))),
        "adapter_up_maps": scatter_about(key_of[6], (ADAPTER_TOTAL, ADAPTER_RANK, MODEL_WIDTH), ADAPTER_RANK ** -0.5, 0.75, ((0, 16), (2, 32))),
        "tenant_adapter_slot": draw_tenant_adapter_slot(jax.random.fold_in(key_of[9], 71), 0),
        "tenant_per_block": draw_tenant_per_block(jax.random.fold_in(key_of[9], 71), 0),
    }


adapter_scale = 0.5
big_negative = -1e30


def group_layer_output(entry_list, output_projection_weight, adapter_down_maps, adapter_up_maps, tenant_adapter_slot):
    q_group, k_group, v_group, lengths, tenants = entry_list
    group_token_count = q_group.shape[0]
    group_size = HQ // KVH
    q_heads = q_group.astype(jnp.float32).reshape(group_token_count, KVH, group_size, HS)
    k_heads = k_group.astype(jnp.float32).reshape(group_token_count, KVH, HS)
    v_heads = v_group.astype(jnp.float32).reshape(group_token_count, KVH, HS)
    prompt_ends = jnp.cumsum(lengths).astype(jnp.int32)
    prompt_starts = prompt_ends - lengths
    positions = jnp.arange(group_token_count, dtype=jnp.int32)
    prompt_ids = jnp.sum((positions[:, None] >= prompt_ends[None, :]).astype(jnp.int32), axis=1)
    prompt_first = prompt_starts[prompt_ids]
    allowed = (positions[None, :] <= positions[:, None]) & (positions[None, :] >= prompt_first[:, None])
    scores = jnp.einsum("ikgd,jkd->kgij", q_heads, k_heads) * (HS ** -0.5)
    scores = jnp.where(allowed[None, None], scores, big_negative)
    row_peak = jnp.max(scores, axis=-1, keepdims=True)
    weights = jnp.exp(scores - row_peak)
    attn_probs = (weights / jnp.sum(weights, axis=-1, keepdims=True)).astype(jnp.bfloat16)
    attended = jnp.einsum("kgij,jkd->ikgd", attn_probs.astype(jnp.float32), v_heads)
    attended = attended.astype(jnp.bfloat16).reshape(group_token_count, HQ * HS)
    feat_width = OUTPUT_FEATURES // N_TP
    slot_identifiers = tenant_adapter_slot[tenants]
    picked_down_map = adapter_down_maps[slot_identifiers]
    picked_up_map = adapter_up_maps[slot_identifiers]
    input_blocks = attended.reshape(BLOCKS, BLOCK, OUTPUT_FEATURES)
    base_projection_sum = jnp.zeros((group_token_count, MODEL_WIDTH), jnp.float32)
    reduced_rank_rows = jnp.zeros((BLOCKS, BLOCK, ADAPTER_RANK), jnp.float32)
    for shard in range(N_TP):
        column_begin = shard * feat_width
        column_end = column_begin + feat_width
        part_out = jnp.dot(attended[:, column_begin:column_end], output_projection_weight[column_begin:column_end], preferred_element_type=jnp.float32)
        base_projection_sum = base_projection_sum + lax.optimization_barrier(part_out.astype(jnp.bfloat16)).astype(jnp.float32)
        adapter_portion = jnp.einsum("typ,tdp->tyd", input_blocks[:, :, column_begin:column_end].astype(jnp.float32), picked_down_map[:, :, column_begin:column_end].astype(jnp.float32))
        reduced_rank_rows = reduced_rank_rows + lax.optimization_barrier(adapter_portion.astype(jnp.bfloat16)).astype(jnp.float32)
    reduced_rank_rows = reduced_rank_rows.astype(jnp.bfloat16)
    adapter_delta = jnp.einsum("vaj,vjt->vat", reduced_rank_rows.astype(jnp.float32), picked_up_map.astype(jnp.float32)).reshape(group_token_count, MODEL_WIDTH)
    return (base_projection_sum + adapter_scale * adapter_delta).astype(jnp.bfloat16)


def reference(queries, rotated_key_rows, values, packed_prompt_length, output_projection_weight, adapter_down_maps, adapter_up_maps, tenant_adapter_slot, tenant_per_block):
    entry_list = (queries.reshape(GROUPS, TOKENS, OUTPUT_FEATURES), rotated_key_rows.reshape(GROUPS, TOKENS, KVH * HS), values.reshape(GROUPS, TOKENS, KVH * HS), packed_prompt_length, tenant_per_block)
    adapted_layer_output = lax.map(lambda group_entries: group_layer_output(group_entries, output_projection_weight, adapter_down_maps, adapter_up_maps, tenant_adapter_slot), entry_list)
    return adapted_layer_output.reshape(GROUPS * TOKENS, MODEL_WIDTH)
```

```python
import functools

import jax
import jax.numpy as jnp
from jax import lax
from jax.experimental import pallas as pl
from jax.experimental.pallas import tpu as pltpu
from jax.sharding import PartitionSpec as P

HS = 128
RANK = 64
BLOCK = 128
BLOCKS = 5
NSP = 4
NTP = 8
NCHIP = 4
NZ = 8
SLOTS = 4
HEADS = 8
ROWS = 160
HALF = 80
FEAT = 1024
COLS = 2048
SLICE = 256
PARTS = 2
PCOLS = COLS // PARTS
TILE = 256

adapter_scale = 0.5
big_negative = -1e30
MESH = pl.DeviceIdType.MESH
F32 = jnp.float32
BF16 = jnp.bfloat16


def copy_to(src, dst, ssem, rsem, **axis):
    return pltpu.make_async_remote_copy(
        src_ref=src, dst_ref=dst, send_sem=ssem, recv_sem=rsem, device_id=axis, device_id_type=MESH
    )


def kernel(
    tas, tpb, plen, q_hbm, k_hbm, v_hbm, w_hbm, dn_hbm, up_hbm, out_ref,
    qv, kv, vv, wv, dnv, upv, att, keep, sibs, sibr, xs, xr, fin,
    zs, zr0, zr1, cross, crossr, down, up2own, up2, lsibs, lkeep, lsibr, lxs, lxr, lrs, lrr,
    lsem, kvs, kvr, atts, attr, zss, zrs, crs, crr, ups, upr,
    sbs, sbr, xss, xrs, lbs, lbr, lxss, lxrs, lys, lyr,
):
    sp = lax.axis_index("sp")
    tp = lax.axis_index("tp")
    grp = lax.axis_index("grp")
    chip = tp // 2
    core = tp % 2
    sib = tp + 1 - 2 * core
    y_lo = grp // NZ
    z = grp % NZ
    other = (1 - y_lo) * NZ + z
    zr = (zr0, zr1)
    right = (sp + 1) % NSP
    left = (sp + NSP - 1) % NSP

    loads = [
        pltpu.make_async_copy(q_hbm, qv, lsem.at[0]),
        pltpu.make_async_copy(k_hbm, kv.at[2], lsem.at[1]),
        pltpu.make_async_copy(v_hbm, vv.at[2], lsem.at[2]),
        pltpu.make_async_copy(dn_hbm, dnv, lsem.at[3]),
        pltpu.make_async_copy(up_hbm, upv, lsem.at[4]),
        pltpu.make_async_copy(w_hbm, wv, lsem.at[5]),
    ]
    barrier = pltpu.get_barrier_semaphore()
    for i in range(1, NSP):
        pl.semaphore_signal(barrier, inc=1, device_id={"sp": (sp + i) % NSP}, device_id_type=MESH)
    for i in range(1, NTP):
        pl.semaphore_signal(barrier, inc=1, device_id={"tp": (tp + i) % NTP}, device_id_type=MESH)
    for i in range(1, NZ):
        pl.semaphore_signal(barrier, inc=1, device_id={"grp": y_lo * NZ + (z + i) % NZ}, device_id_type=MESH)
    pl.semaphore_signal(barrier, inc=1, device_id={"grp": other}, device_id_type=MESH)
    for c in loads:
        c.start()
    pl.semaphore_wait(barrier, (NSP - 1) + (NTP - 1) + (NZ - 1) + 1)

    def kv_copies(i):
        to = (sp + i) % NSP
        return [
            copy_to(k_hbm, kv.at[2 - i], kvs.at[0, i - 1], kvr.at[0, i - 1], sp=to),
            copy_to(v_hbm, vv.at[2 - i], kvs.at[1, i - 1], kvr.at[1, i - 1], sp=to),
        ]

    for i in (1, 2):
        @pl.when(sp + i < NSP)
        def _(i=i):
            for c in kv_copies(i):
                c.start()

    loads[3].wait()
    loads[4].wait()

    def slot_of(g, b):
        return tas[tpb[g, b]]

    def pack(t, carry):
        g = t
        pick = jnp.int32(0)
        for b in range(BLOCKS):
            slot = slot_of(g, b)
            pick = pick + jnp.where(slot // SLOTS == grp, slot % SLOTS, 0)
        zs[0, g % NZ, g // NZ] = dnv[pick]
        zs[1, g % NZ, g // NZ] = upv[pick]
        return carry

    lax.fori_loop(0, 2 * NZ, pack, 0)

    def z_copy(m, i):
        to = (z + i) % NZ
        return copy_to(zs.at[m, to], zr[m].at[z], zss.at[m, i - 1], zrs.at[m, i - 1], grp=y_lo * NZ + to)

    for m in range(2):
        for i in range(1, NZ):
            z_copy(m, i).start()
        for j in range(2):
            zr[m][z, j] = zs[m, z, j]

    for c in loads[:3]:
        c.wait()
    for i in (1, 2):
        @pl.when(sp >= i)
        def _(i=i):
            for c in kv_copies(i):
                c.wait_recv()

        @pl.when(sp < i)
        def _(i=i):
            kv[2 - i] = jnp.zeros((ROWS, HS), BF16)
            vv[2 - i] = jnp.zeros((ROWS, HS), BF16)

    end0 = plen[0, 0]
    end1 = end0 + plen[0, 1]
    keys = kv[...].reshape(3 * ROWS, HS)
    vals = vv[...].reshape(3 * ROWS, HS)

    def att_copy(h, to_right):
        k = 1 if (h == 0) == to_right else 3
        slot = 0 if k == 1 else 1
        dst_row = h
        side = 0 if to_right else 1
        return copy_to(
            att.at[0, h], att.at[k, dst_row], atts.at[side, slot], attr.at[side, slot],
            sp=right if to_right else left,
        )

    for h in range(2):
        qpos = sp * ROWS + h * HALF + lax.broadcasted_iota(jnp.int32, (HALF, 3 * ROWS), 0)
        kpos = (sp - 2) * ROWS + lax.broadcasted_iota(jnp.int32, (HALF, 3 * ROWS), 1)
        first = jnp.where(qpos >= end1, end1, jnp.where(qpos >= end0, end0, 0))
        allowed = (kpos <= qpos) & (kpos >= first)
        for n in range(HEADS):
            qh = qv[h * HALF:(h + 1) * HALF, n * HS:(n + 1) * HS]
            s = lax.dot_general(qh, keys, (((1,), (1,)), ((), ())), preferred_element_type=F32)
            s = jnp.where(allowed, s * HS ** -0.5, big_negative)
            p = jnp.exp(s - jnp.max(s, axis=1, keepdims=True))
            total = jnp.sum(p, axis=1, keepdims=True)
            o = jnp.dot(p.astype(BF16), vals, preferred_element_type=F32)
            att[0, h, :, n * HS:(n + 1) * HS] = (o / total).astype(BF16)
        if h == 0:
            att_copy(0, True).start()
        else:
            att_copy(1, False).start()
            att_copy(1, True).start()
            att_copy(0, False).start()
    loads[5].wait()

    relays = [
        copy_to(att.at[1, 0], att.at[2, 0], atts.at[0, 2], attr.at[0, 2], sp=right),
        copy_to(att.at[1, 1], att.at[2, 1], atts.at[1, 2], attr.at[1, 2], sp=left),
    ]

    shift = 2 * core - 1
    keep_block = [sp, (sp + NSP + shift) % NSP, (sp + 2) % NSP, (sp + NSP - shift) % NSP]

    def sib_copy(k, part):
        cols = pl.ds(part * PCOLS, PCOLS)
        return copy_to(sibs.at[k, :, cols], sibr.at[k, :, cols], sbs.at[k, part], sbr.at[k, part], tp=sib)

    def product(k):
        rows = att.at[k]
        for part in range(PARTS):
            def tile(n, carry, part=part):
                cols = pl.ds(pl.multiple_of(part * PCOLS + n * TILE, TILE), TILE)
                v = jnp.dot(
                    rows[...].reshape(ROWS, FEAT), wv[:, cols], preferred_element_type=F32
                )
                keep[k, :, cols] = jnp.where(core == 0, v[:HALF], v[HALF:])
                sibs[k, :, cols] = jnp.where(core == 0, v[HALF:], v[:HALF]).astype(BF16)
                return carry

            lax.fori_loop(0, PCOLS // TILE, tile, 0)
            sib_copy(k, part).start()

    def x_copy(k, part):
        cols = pl.ds(part * PCOLS, PCOLS)
        rel = (chip + NCHIP - keep_block[k] + NCHIP - 1) % NCHIP
        return copy_to(
            xs.at[k, :, cols], xr.at[rel, :, cols], xss.at[k, part], xrs.at[rel, part],
            tp=2 * keep_block[k] + core,
        )

    def x_phase(k):
        for part in range(PARTS):
            cols = pl.ds(part * PCOLS, PCOLS)
            sib_copy(k, part).wait_recv()
            total = keep[k, :, cols] + sibr[k, :, cols].astype(F32)

            @pl.when(keep_block[k] == chip)
            def _():
                fin[:, cols] = total

            @pl.when(keep_block[k] != chip)
            def _():
                xs[k, :, cols] = total.astype(BF16)
                x_copy(k, part).start()

    product(0)

    for side in range(2):
        if side == 0:
            att_copy(0, True).wait_recv()
        else:
            att_copy(1, False).wait_recv()
        relays[side].start()
    x_phase(0)
    product(1)

    def cross_copy(m):
        return copy_to(cross.at[m], crossr.at[m], crs.at[m], crr.at[m], grp=other)

    def cross_send(m):
        for i in range(1, NZ):
            z_copy(m, i).wait_recv()

        def fill(b, carry):
            owner = slot_of(other, b) // SLOTS
            cross[m, b] = zr[m][owner % NZ, 1 - y_lo]
            return carry

        lax.fori_loop(0, BLOCKS, fill, 0)
        cross_copy(m).start()

    def cross_take(m, dst):
        cross_copy(m).wait_recv()

        def fill(b, carry):
            owner = slot_of(grp, b) // SLOTS
            dst[b] = jnp.where(owner // NZ == y_lo, zr[m][owner % NZ, y_lo], crossr[m, b])
            return carry

        lax.fori_loop(0, BLOCKS, fill, 0)

    cross_send(0)
    x_phase(1)
    cross_send(1)

    for side in range(2):
        relays[side].wait_recv()
    product(2)
    cross_take(0, down)
    cross_take(1, up2own)

    def up_copy(i):
        to = (tp + i) % NTP
        return copy_to(up2own.at[pl.ds(to // 2, 2)], up2.at[tp], ups.at[i - 1], upr.at[i - 1], tp=to)

    for i in range(1, NTP):
        up_copy(i).start()
    up2[tp] = up2own[pl.ds(chip, 2)]
    x_phase(2)

    att_copy(0, False).wait_recv()
    att_copy(1, True).wait_recv()

    lane = lax.broadcasted_iota(jnp.int32, (HALF, 2 * RANK), 1)
    row = lax.broadcasted_iota(jnp.int32, (HALF, 2 * RANK), 0)
    features = pl.ds(pl.multiple_of(sp * SLICE, SLICE), SLICE)
    blocks_of = [(sp, sp), (left, right), ((sp + 2) % NSP,) * 2, (right, left)]
    for k in range(4):
        halves = []
        for h in range(2):
            sb = blocks_of[k][h]
            pair = down[pl.ds(sb, 2)].reshape(2 * RANK, SLICE)
            lr = lax.dot_general(
                att[k, h, :, features], pair, (((1,), (1,)), ((), ())), preferred_element_type=F32
            )
            early = (row + h * HALF < BLOCK - (ROWS - BLOCK) * sb).astype(jnp.int32)
            firsts = (lane < RANK).astype(jnp.int32)
            halves.append(jnp.where(early == firsts, lr, 0.0))
        lkeep[k] = jnp.where(core == 0, halves[0], halves[1])
        lsibs[k] = jnp.where(core == 0, halves[1], halves[0]).astype(BF16)
    lsib_copy = copy_to(lsibs, lsibr, lbs, lbr, tp=sib)
    lsib_copy.start()

    product(3)

    def lx_copy(k):
        rel = (chip + NCHIP - keep_block[k] + NCHIP - 1) % NCHIP
        return copy_to(
            lxs.at[k], lxr.at[rel], lxss.at[k], lxrs.at[rel], tp=2 * keep_block[k] + core
        )

    lsib_copy.wait_recv()
    for k in range(4):
        total = lkeep[k] + lsibr[k].astype(F32)

        @pl.when(keep_block[k] == chip)
        def _():
            lrs[...] = total

        @pl.when(keep_block[k] != chip)
        def _():
            lxs[k] = total.astype(BF16)
            lx_copy(k).start()

    x_phase(3)

    for rel in range(NCHIP - 1):
        copy_to(lxs.at[0], lxr.at[rel], lxss.at[0], lxrs.at[rel], tp=sib).wait_recv()
    lrs[...] = lrs[...] + (lxr[0].astype(F32) + lxr[1].astype(F32) + lxr[2].astype(F32))

    def ly_copy(i):
        return copy_to(lrs, lrr.at[i - 1], lys.at[i - 1], lyr.at[i - 1], sp=(sp + i) % NSP)

    for i in range(1, NSP):
        ly_copy(i).start()
    for i in range(1, NTP):
        up_copy(i).wait_recv()
    for i in range(1, NSP):
        ly_copy(i).wait_recv()
    low = (lrs[...] + (lrr[0] + lrr[1] + lrr[2])).astype(BF16)
    for part in range(PARTS):
        cols = pl.ds(part * PCOLS, PCOLS)
        for rel in range(NCHIP - 1):
            copy_to(
                xs.at[0, :, cols], xr.at[rel, :, cols], xss.at[0, part], xrs.at[rel, part], tp=sib
            ).wait_recv()
        for n in range(PCOLS // SLICE):
            j = part * (PCOLS // SLICE) + n
            c = pl.ds(j * SLICE, SLICE)
            delta = jnp.dot(low, up2[j].reshape(2 * RANK, SLICE), preferred_element_type=F32)
            base = fin[:, c] + (
                xr[0, :, c].astype(F32) + xr[1, :, c].astype(F32) + xr[2, :, c].astype(F32)
            )
            out_ref[:, c] = (base + adapter_scale * delta).astype(BF16)

    for i in (1, 2):
        @pl.when(sp + i < NSP)
        def _(i=i):
            for c in kv_copies(i):
                c.wait_send()
    for m in range(2):
        for i in range(1, NZ):
            z_copy(m, i).wait_send()
        cross_copy(m).wait_send()
    for h in range(2):
        for to_right in (True, False):
            att_copy(h, to_right).wait_send()
    for r in relays:
        r.wait_send()
    for i in range(1, NTP):
        up_copy(i).wait_send()
    lsib_copy.wait_send()
    for k in range(4):
        for part in range(PARTS):
            sib_copy(k, part).wait_send()

        @pl.when(keep_block[k] != chip)
        def _():
            lx_copy(k).wait_send()
            for part in range(PARTS):
                x_copy(k, part).wait_send()
    for i in range(1, NSP):
        ly_copy(i).wait_send()


def on_device(q, k, v, plen, w, dn, up, tas, tpb):
    smem = pl.BlockSpec(memory_space=pltpu.SMEM)
    anym = pl.BlockSpec(memory_space=pl.ANY)
    V = pltpu.VMEM
    D = pltpu.SemaphoreType.DMA
    return pl.pallas_call(
        kernel,
        out_shape=jax.ShapeDtypeStruct((HALF, COLS), BF16),
        in_specs=[smem] * 3 + [anym] * 6,
        out_specs=pl.BlockSpec(memory_space=pltpu.VMEM),
        scratch_shapes=[
            V((ROWS, FEAT), BF16),
            V((3, ROWS, HS), BF16),
            V((3, ROWS, HS), BF16),
            V((FEAT, COLS), BF16),
            V((SLOTS, RANK, SLICE), BF16),
            V((SLOTS, RANK, SLICE), BF16),
            V((4, 2, HALF, FEAT), BF16),
            V((4, HALF, COLS), F32),
            V((4, HALF, COLS), BF16),
            V((4, HALF, COLS), BF16),
            V((4, HALF, COLS), BF16),
            V((NCHIP - 1, HALF, COLS), BF16),
            V((HALF, COLS), F32),
            V((2, NZ, 2, RANK, SLICE), BF16),
            V((NZ, 2, RANK, SLICE), BF16),
            V((NZ, 2, RANK, SLICE), BF16),
            V((2, BLOCKS, RANK, SLICE), BF16),
            V((2, BLOCKS, RANK, SLICE), BF16),
            V((BLOCKS, RANK, SLICE), BF16),
            V((BLOCKS, RANK, SLICE), BF16),
            V((NTP, 2, RANK, SLICE), BF16),
            V((4, HALF, 2 * RANK), BF16),
            V((4, HALF, 2 * RANK), F32),
            V((4, HALF, 2 * RANK), BF16),
            V((4, HALF, 2 * RANK), BF16),
            V((NCHIP - 1, HALF, 2 * RANK), BF16),
            V((HALF, 2 * RANK), F32),
            V((NSP - 1, HALF, 2 * RANK), F32),
            D((6,)),
            D((2, 2)), D((2, 2)),
            D((2, 3)), D((2, 3)),
            D((2, NZ - 1)), D((2, NZ - 1)),
            D((2,)), D((2,)),
            D((NTP - 1,)), D((NTP - 1,)),
            D((4, PARTS)), D((4, PARTS)),
            D((4, PARTS)), D((NCHIP - 1, PARTS)),
            D, D,
            D((4,)), D((NCHIP - 1,)),
            D((NSP - 1,)), D((NSP - 1,)),
        ],
        compiler_params=pltpu.CompilerParams(
            collective_id=0, has_side_effects=True, vmem_limit_bytes=56 * 1024 * 1024
        ),
    )(tas, tpb, plen, q, k, v, w, dn, up)


def solution(mesh):
    return jax.shard_map(
        on_device,
        mesh=mesh,
        in_specs=(
            P(("grp", "sp"), "tp"),
            P(("grp", "sp"), "tp"),
            P(("grp", "sp"), "tp"),
            P("grp", None),
            P("tp", "sp"),
            P("grp", None, ("tp", "sp")),
            P("grp", None, ("sp", "tp")),
            P(),
            P(),
        ),
        out_specs=P(("grp", "tp"), "sp"),
        check_vma=False,
    )
```

```python
import functools

import jax
import jax.numpy as jnp
from jax import lax
from jax.experimental import pallas as pl
from jax.experimental.pallas import tpu as pltpu
from jax.sharding import PartitionSpec as P

HS = 128
RANK = 64
BLOCK = 128
BLOCKS = 5
NSP = 4
NTP = 8
NCHIP = 4
NZ = 8
SLOTS = 4
HEADS = 8
ROWS = 160
HALF = 80
FEAT = 1024
COLS = 2048
SLICE = 256
PARTS = 4
PCOLS = COLS // PARTS
TILE = 256
STACK = 8
PIECES = ((0, 32), (32, 48))

adapter_scale = 0.5
big_negative = -1e30
MESH = pl.DeviceIdType.MESH
F32 = jnp.float32
BF16 = jnp.bfloat16


def copy_to(src, dst, ssem, rsem, **axis):
    return pltpu.make_async_remote_copy(
        src_ref=src, dst_ref=dst, send_sem=ssem, recv_sem=rsem, device_id=axis, device_id_type=MESH
    )


def kernel(
    tas, tpb, plen, q_hbm, k_hbm, v_hbm, w_hbm, dn_hbm, up_hbm, out_ref,
    qv, kv, vv, wv, dnv, upv, probs, att, keep, sibs, sibr, xs, xr, fin,
    zs, zr0, zr1, cross, crossr, down, up2own, up2, lxs, lxr, lrs, lrr,
    lsem, kvs, kvr, atts, attr, zss, zrs, crs, crr, ups, upr,
    sbs, sbr, xss, xrs, lxss, lxrs, lys, lyr,
):
    sp = lax.axis_index("sp")
    tp = lax.axis_index("tp")
    grp = lax.axis_index("grp")
    chip = tp // 2
    core = tp % 2
    sib = tp + 1 - 2 * core
    y_lo = grp // NZ
    z = grp % NZ
    other = (1 - y_lo) * NZ + z
    zr = (zr0, zr1)
    right = (sp + 1) % NSP
    left = (sp + NSP - 1) % NSP

    loads = [
        pltpu.make_async_copy(k_hbm, kv.at[2], lsem.at[0]),
        pltpu.make_async_copy(q_hbm, qv, lsem.at[1]),
        pltpu.make_async_copy(v_hbm, vv.at[2], lsem.at[2]),
        pltpu.make_async_copy(dn_hbm, dnv, lsem.at[3]),
        pltpu.make_async_copy(up_hbm, upv, lsem.at[4]),
        pltpu.make_async_copy(w_hbm, wv, lsem.at[5]),
    ]
    barrier = pltpu.get_barrier_semaphore()
    for i in range(1, NSP):
        pl.semaphore_signal(barrier, inc=1, device_id={"sp": (sp + i) % NSP}, device_id_type=MESH)
    for i in range(1, NTP):
        pl.semaphore_signal(barrier, inc=1, device_id={"tp": (tp + i) % NTP}, device_id_type=MESH)
    for i in range(1, NZ):
        pl.semaphore_signal(barrier, inc=1, device_id={"grp": y_lo * NZ + (z + i) % NZ}, device_id_type=MESH)
    pl.semaphore_signal(barrier, inc=1, device_id={"grp": other}, device_id_type=MESH)
    for c in loads:
        c.start()
    pl.semaphore_wait(barrier, (NSP - 1) + (NTP - 1) + (NZ - 1) + 1)

    def kv_copy(m, i):
        return copy_to(
            (k_hbm, v_hbm)[m], (kv, vv)[m].at[2 - i], kvs.at[m, i - 1], kvr.at[m, i - 1],
            sp=(sp + i) % NSP,
        )

    for m in range(2):
        for i in (1, 2):
            @pl.when(sp + i < NSP)
            def _():
                kv_copy(m, i).start()

    loads[3].wait()
    loads[4].wait()

    def slot_of(g, b):
        return tas[tpb[b, g]]

    def pack(g, carry):
        pick = jnp.int32(0)
        for b in range(BLOCKS):
            slot = slot_of(g, b)
            pick = pick + jnp.where(slot // SLOTS == grp, slot % SLOTS, 0)
        zs[0, g % NZ, g // NZ] = dnv[pick]
        zs[1, g % NZ, g // NZ] = upv[pick]
        return carry

    lax.fori_loop(0, 2 * NZ, pack, 0)

    def z_copy(m, i):
        to = (z + i) % NZ
        return copy_to(
            zs.at[m, to], zr[m].at[z], zss.at[m, i - 1], zrs.at[m, i - 1], grp=y_lo * NZ + to
        )

    for m in range(2):
        for i in range(1, NZ):
            z_copy(m, i).start()
        for j in range(2):
            zr[m][z, j] = zs[m, z, j]

    def kv_ready(m):
        for i in (1, 2):
            @pl.when(sp >= i)
            def _():
                kv_copy(m, i).wait_recv()

            @pl.when(sp < i)
            def _():
                (kv, vv)[m][2 - i] = jnp.zeros((ROWS, HS), BF16)

    loads[0].wait()
    loads[1].wait()
    kv_ready(0)
    end0 = plen[0, 0]
    end1 = end0 + plen[0, 1]
    keys = kv[...].reshape(3 * ROWS, HS)
    for h in range(2):
        qpos = sp * ROWS + h * HALF + lax.broadcasted_iota(jnp.int32, (HALF, 3 * ROWS), 0)
        kpos = (sp - 2) * ROWS + lax.broadcasted_iota(jnp.int32, (HALF, 3 * ROWS), 1)
        first = jnp.where(qpos >= end1, end1, jnp.where(qpos >= end0, end0, 0))
        allowed = (kpos <= qpos) & (kpos >= first)
        for n in range(0, HEADS, STACK):
            qh = jnp.concatenate(
                [qv[h * HALF:(h + 1) * HALF, m * HS:(m + 1) * HS] for m in range(n, n + STACK)], axis=0
            )
            s = lax.dot_general(qh, keys, (((1,), (1,)), ((), ())), preferred_element_type=F32)
            s = jnp.where(
                allowed[None], s.reshape(STACK, HALF, 3 * ROWS) * HS ** -0.5, big_negative
            )
            p = jnp.exp(s - jnp.max(s, axis=2, keepdims=True))
            probs[h, n * HALF:(n + STACK) * HALF] = p.astype(BF16).reshape(STACK * HALF, 3 * ROWS)
    loads[2].wait()
    kv_ready(1)
    vals = jnp.concatenate(
        [vv[...].reshape(3 * ROWS, HS), jnp.ones((3 * ROWS, HS), BF16)], axis=1
    )

    def first_copy(side):
        return copy_to(
            att.at[0, side], att.at[1, side], atts.at[side, 0], attr.at[side, 0],
            sp=(right, left)[side],
        )

    def later_copy(side, piece):
        rows = pl.ds(*PIECES[piece])
        return copy_to(
            att.at[0, 1 - side, rows], att.at[3, 1 - side, rows],
            atts.at[side, 1 + piece], attr.at[side, 1 + piece],
            sp=(right, left)[side],
        )

    def relay(side):
        return copy_to(
            att.at[1, side], att.at[2, side], atts.at[side, 3], attr.at[side, 3],
            sp=(right, left)[side],
        )

    for h in range(2):
        for n in range(0, HEADS, STACK):
            o = jnp.dot(
                probs[h, n * HALF:(n + STACK) * HALF], vals, preferred_element_type=F32
            )
            o = (o[:, :HS] / o[:, HS:]).astype(BF16)
            for m in range(STACK):
                att[0, h, :, (n + m) * HS:(n + m + 1) * HS] = o[m * HALF:(m + 1) * HALF]
        first_copy(h).start()
    for side in range(2):
        later_copy(side, 0).start()
    loads[5].wait()

    shift = 2 * core - 1
    keep_block = [sp, (sp + NSP + shift) % NSP, (sp + 2) % NSP, (sp + NSP - shift) % NSP]

    def sib_copy(k, part):
        cols = pl.ds(part * PCOLS, PCOLS)
        return copy_to(sibs.at[k, :, cols], sibr.at[k, :, cols], sbs.at[k, part], sbr.at[k, part], tp=sib)

    def product(k):
        for part in range(PARTS):
            for n in range(PCOLS // TILE):
                cols = pl.ds(part * PCOLS + n * TILE, TILE)
                v = jnp.dot(
                    att[k].reshape(ROWS, FEAT), wv[:, cols], preferred_element_type=F32
                )
                keep[k, :, cols] = jnp.where(core == 0, v[:HALF], v[HALF:])
                sibs[k, :, cols] = jnp.where(core == 0, v[HALF:], v[:HALF]).astype(BF16)
            sib_copy(k, part).start()

    def x_copy(k, part):
        cols = pl.ds(part * PCOLS, PCOLS)
        rel = (chip + NCHIP - keep_block[k] + NCHIP - 1) % NCHIP
        return copy_to(
            xs.at[k, :, cols], xr.at[rel, :, cols], xss.at[k, part], xrs.at[rel, part],
            tp=2 * keep_block[k] + core,
        )

    def x_phase(k):
        for part in range(PARTS):
            cols = pl.ds(part * PCOLS, PCOLS)
            sib_copy(k, part).wait_recv()
            total = keep[k, :, cols] + sibr[k, :, cols].astype(F32)

            @pl.when(keep_block[k] == chip)
            def _():
                fin[:, cols] = total

            @pl.when(keep_block[k] != chip)
            def _():
                xs[k, :, cols] = total.astype(BF16)
                x_copy(k, part).start()

    lane = lax.broadcasted_iota(jnp.int32, (HALF, 2 * RANK), 1)
    row = lax.broadcasted_iota(jnp.int32, (HALF, 2 * RANK), 0)
    features = pl.ds(pl.multiple_of(sp * SLICE, SLICE), SLICE)
    far = (sp + 2) % NSP
    blocks_of = [(sp, sp), (left, right), (far, far), (right, left)]

    def low_copy(k, h):
        to = 2 * blocks_of[k][h] + h
        rel = (tp + NTP - to + NTP - 1) % NTP
        return copy_to(lxs.at[k, h], lxr.at[rel], lxss.at[k, h], lxrs.at[rel], tp=to)

    def low_rank(k):
        for h in range(2):
            sb = blocks_of[k][h]
            pair = down[pl.ds(sb, 2)].reshape(2 * RANK, SLICE)
            lr = lax.dot_general(
                att[k, h, :, features], pair, (((1,), (1,)), ((), ())), preferred_element_type=F32
            )
            early = (row + h * HALF < BLOCK - (ROWS - BLOCK) * sb).astype(jnp.int32)
            firsts = (lane < RANK).astype(jnp.int32)
            lr = jnp.where(early == firsts, lr, 0.0)

            @pl.when(2 * sb + h == tp)
            def _():
                lrs[...] = lr

            @pl.when(2 * sb + h != tp)
            def _():
                lxs[k, h] = lr.astype(BF16)
                low_copy(k, h).start()

    def cross_copy(m):
        return copy_to(cross.at[m], crossr.at[m], crs.at[m], crr.at[m], grp=other)

    def cross_send(m):
        for i in range(1, NZ):
            z_copy(m, i).wait_recv()

        def fill(b, carry):
            owner = slot_of(other, b) // SLOTS
            cross[m, b] = zr[m][owner % NZ, 1 - y_lo]
            return carry

        lax.fori_loop(0, BLOCKS, fill, 0)
        cross_copy(m).start()

    def cross_take(m, dst):
        cross_copy(m).wait_recv()

        def fill(b, carry):
            owner = slot_of(grp, b) // SLOTS
            dst[b] = jnp.where(owner // NZ == y_lo, zr[m][owner % NZ, y_lo], crossr[m, b])
            return carry

        lax.fori_loop(0, BLOCKS, fill, 0)

    def up_copy(i):
        to = (chip + i) % NCHIP
        return copy_to(
            up2own.at[pl.ds(to, 2)], up2.at[tp], ups.at[i - 1], upr.at[i - 1], tp=2 * to + core
        )

    def up_share(i):
        at = 2 * ((chip + NCHIP - i) % NCHIP) + core
        return copy_to(
            up2.at[at], up2.at[at], ups.at[NCHIP - 1 + i], upr.at[NCHIP - 1 + i], tp=sib
        )

    product(0)

    for side in range(2):
        first_copy(side).wait_recv()
        relay(side).start()
    for side in range(2):
        later_copy(side, 1).start()
    x_phase(0)
    product(1)
    cross_send(0)
    x_phase(1)

    for side in range(2):
        relay(side).wait_recv()
    product(2)
    cross_take(0, down)
    for k in range(3):
        low_rank(k)
    x_phase(2)
    cross_send(1)

    for side in range(2):
        for piece in range(2):
            later_copy(side, piece).wait_recv()
    low_rank(3)
    product(3)
    cross_take(1, up2own)
    for i in range(1, NCHIP):
        up_copy(i).start()
    up2[tp] = up2own[pl.ds(chip, 2)]
    up_share(0).start()
    x_phase(3)

    for rel in range(NTP - 1):
        copy_to(lxs.at[0, 0], lxr.at[rel], lxss.at[0, 0], lxrs.at[rel], tp=sib).wait_recv()
    low = lrs[...]
    for rel in range(NTP - 1):
        low = low + lxr[rel].astype(F32)
    lrs[...] = low

    def ly_copy(i):
        return copy_to(lrs, lrr.at[i - 1], lys.at[i - 1], lyr.at[i - 1], sp=(sp + i) % NSP)

    for i in range(1, NSP):
        ly_copy(i).start()
    for i in range(1, NCHIP):
        up_copy(i).wait_recv()
        up_share(i).start()
    for i in range(1, NSP):
        ly_copy(i).wait_recv()
    low = (lrs[...] + (lrr[0] + lrr[1] + lrr[2])).astype(BF16)
    for i in range(NCHIP):
        up_share(i).wait_recv()
    for part in range(PARTS):
        cols = pl.ds(part * PCOLS, PCOLS)
        for rel in range(NCHIP - 1):
            copy_to(
                xs.at[0, :, cols], xr.at[rel, :, cols], xss.at[0, part], xrs.at[rel, part], tp=sib
            ).wait_recv()
        for n in range(PCOLS // SLICE):
            j = part * (PCOLS // SLICE) + n
            c = pl.ds(j * SLICE, SLICE)
            delta = jnp.dot(low, up2[j].reshape(2 * RANK, SLICE), preferred_element_type=F32)
            base = fin[:, c] + (
                xr[0, :, c].astype(F32) + xr[1, :, c].astype(F32) + xr[2, :, c].astype(F32)
            )
            out_ref[:, c] = (base + adapter_scale * delta).astype(BF16)

    for m in range(2):
        for i in (1, 2):
            @pl.when(sp + i < NSP)
            def _():
                kv_copy(m, i).wait_send()
        for i in range(1, NZ):
            z_copy(m, i).wait_send()
        cross_copy(m).wait_send()
    for side in range(2):
        first_copy(side).wait_send()
        relay(side).wait_send()
        for piece in range(2):
            later_copy(side, piece).wait_send()
    for i in range(1, NCHIP):
        up_copy(i).wait_send()
    for i in range(NCHIP):
        up_share(i).wait_send()
    for k in range(4):
        for part in range(PARTS):
            sib_copy(k, part).wait_send()

        @pl.when(keep_block[k] != chip)
        def _():
            for part in range(PARTS):
                x_copy(k, part).wait_send()

        for h in range(2):
            @pl.when(2 * blocks_of[k][h] + h != tp)
            def _():
                low_copy(k, h).wait_send()
    for i in range(1, NSP):
        ly_copy(i).wait_send()


def on_device(q, k, v, plen, w, dn, up, tas, tpb):
    smem = pl.BlockSpec(memory_space=pltpu.SMEM)
    anym = pl.BlockSpec(memory_space=pl.ANY)
    V = pltpu.VMEM
    D = pltpu.SemaphoreType.DMA
    return pl.pallas_call(
        kernel,
        out_shape=jax.ShapeDtypeStruct((HALF, COLS), BF16),
        in_specs=[smem] * 3 + [anym] * 6,
        out_specs=pl.BlockSpec(memory_space=pltpu.VMEM),
        scratch_shapes=[
            V((ROWS, FEAT), BF16),
            V((3, ROWS, HS), BF16),
            V((3, ROWS, HS), BF16),
            V((FEAT, COLS), BF16),
            V((SLOTS, RANK, SLICE), BF16),
            V((SLOTS, RANK, SLICE), BF16),
            V((2, HEADS * HALF, 3 * ROWS), BF16),
            V((4, 2, HALF, FEAT), BF16),
            V((4, HALF, COLS), F32),
            V((4, HALF, COLS), BF16),
            V((4, HALF, COLS), BF16),
            V((4, HALF, COLS), BF16),
            V((NCHIP - 1, HALF, COLS), BF16),
            V((HALF, COLS), F32),
            V((2, NZ, 2, RANK, SLICE), BF16),
            V((NZ, 2, RANK, SLICE), BF16),
            V((NZ, 2, RANK, SLICE), BF16),
            V((2, BLOCKS, RANK, SLICE), BF16),
            V((2, BLOCKS, RANK, SLICE), BF16),
            V((BLOCKS, RANK, SLICE), BF16),
            V((BLOCKS, RANK, SLICE), BF16),
            V((NTP, 2, RANK, SLICE), BF16),
            V((4, 2, HALF, 2 * RANK), BF16),
            V((NTP - 1, HALF, 2 * RANK), BF16),
            V((HALF, 2 * RANK), F32),
            V((NSP - 1, HALF, 2 * RANK), F32),
            D((6,)),
            D((2, 2)), D((2, 2)),
            D((2, 4)), D((2, 4)),
            D((2, NZ - 1)), D((2, NZ - 1)),
            D((2,)), D((2,)),
            D((2 * NCHIP - 1,)), D((2 * NCHIP - 1,)),
            D((4, PARTS)), D((4, PARTS)),
            D((4, PARTS)), D((NCHIP - 1, PARTS)),
            D((4, 2)), D((NTP - 1,)),
            D((NSP - 1,)), D((NSP - 1,)),
        ],
        compiler_params=pltpu.CompilerParams(
            collective_id=0, has_side_effects=True, vmem_limit_bytes=56 * 1024 * 1024
        ),
    )(tas, tpb.T, plen, q, k, v, w, dn, up)


def solution(mesh):
    return jax.shard_map(
        on_device,
        mesh=mesh,
        in_specs=(
            P(("grp", "sp"), "tp"),
            P(("grp", "sp"), "tp"),
            P(("grp", "sp"), "tp"),
            P("grp", None),
            P("tp", "sp"),
            P("grp", None, ("tp", "sp")),
            P("grp", None, ("sp", "tp")),
            P(),
            P(),
        ),
        out_specs=P(("grp", "tp"), "sp"),
        check_vma=False,
    )
```

```python
import functools

import jax
import jax.numpy as jnp
from jax import lax
from jax.experimental import pallas as pl
from jax.experimental.pallas import tpu as pltpu
from jax.sharding import PartitionSpec as P

HS = 128
RANK = 64
BLOCK = 128
BLOCKS = 5
NSP = 4
NTP = 8
NCHIP = 4
NZ = 8
SLOTS = 4
HEADS = 8
ROWS = 160
HALF = 80
FEAT = 1024
COLS = 2048
SLICE = 256
PARTS = 4
PCOLS = COLS // PARTS
TILE = 256
STACK = 8
PIECES = ((0, 32), (32, 48))

adapter_scale = 0.5
big_negative = -1e30
MESH = pl.DeviceIdType.MESH
F32 = jnp.float32
BF16 = jnp.bfloat16


def copy_to(src, dst, ssem, rsem, **axis):
    return pltpu.make_async_remote_copy(
        src_ref=src, dst_ref=dst, send_sem=ssem, recv_sem=rsem, device_id=axis, device_id_type=MESH
    )


def kernel(
    tas, tpb, plen, q_hbm, k_hbm, v_hbm, w_hbm, dn_hbm, up_hbm, out_ref,
    qv, kv, vv, wv, dnv, upv, probs, att, keep, sibs, sibr, xs, xr, hop, fin,
    zs, zr0, zr1, cross, crossr, down, up2own, up2, lxs, lxr, lrs, lrr,
    lsem, kvs, kvr, atts, attr, zss, zrs, crs, crr, ups, upr,
    sbs, sbr, xss, xrs, txs, txr, lxss, lxrs, lys, lyr,
):
    sp = lax.axis_index("sp")
    tp = lax.axis_index("tp")
    grp = lax.axis_index("grp")
    chip = tp // 2
    core = tp % 2
    sib = tp + 1 - 2 * core
    y_lo = grp // NZ
    z = grp % NZ
    other = (1 - y_lo) * NZ + z
    zr = (zr0, zr1)
    right = (sp + 1) % NSP
    left = (sp + NSP - 1) % NSP

    loads = [
        pltpu.make_async_copy(k_hbm, kv.at[2], lsem.at[0]),
        pltpu.make_async_copy(q_hbm, qv, lsem.at[1]),
        pltpu.make_async_copy(v_hbm, vv.at[2], lsem.at[2]),
        pltpu.make_async_copy(dn_hbm, dnv, lsem.at[3]),
        pltpu.make_async_copy(up_hbm, upv, lsem.at[4]),
        pltpu.make_async_copy(w_hbm, wv, lsem.at[5]),
    ]
    barrier = pltpu.get_barrier_semaphore()
    for i in range(1, NSP):
        pl.semaphore_signal(barrier, inc=1, device_id={"sp": (sp + i) % NSP}, device_id_type=MESH)
    for i in range(1, NTP):
        pl.semaphore_signal(barrier, inc=1, device_id={"tp": (tp + i) % NTP}, device_id_type=MESH)
    for i in range(1, NZ):
        pl.semaphore_signal(barrier, inc=1, device_id={"grp": y_lo * NZ + (z + i) % NZ}, device_id_type=MESH)
    pl.semaphore_signal(barrier, inc=1, device_id={"grp": other}, device_id_type=MESH)
    for c in loads:
        c.start()
    pl.semaphore_wait(barrier, (NSP - 1) + (NTP - 1) + (NZ - 1) + 1)

    def kv_copy(m, i):
        return copy_to(
            (k_hbm, v_hbm)[m], (kv, vv)[m].at[2 - i], kvs.at[m, i - 1], kvr.at[m, i - 1],
            sp=(sp + i) % NSP,
        )

    for m in range(2):
        for i in (1, 2):
            @pl.when(sp + i < NSP)
            def _():
                kv_copy(m, i).start()

    loads[3].wait()
    loads[4].wait()

    def slot_of(g, b):
        return tas[tpb[b, g]]

    def pack(g, carry):
        pick = jnp.int32(0)
        for b in range(BLOCKS):
            slot = slot_of(g, b)
            pick = pick + jnp.where(slot // SLOTS == grp, slot % SLOTS, 0)
        zs[0, g % NZ, g // NZ] = dnv[pick]
        zs[1, g % NZ, g // NZ] = upv[pick]
        return carry

    lax.fori_loop(0, 2 * NZ, pack, 0)

    def z_copy(m, i):
        to = (z + i) % NZ
        return copy_to(
            zs.at[m, to], zr[m].at[z], zss.at[m, i - 1], zrs.at[m, i - 1], grp=y_lo * NZ + to
        )

    for m in range(2):
        for i in range(1, NZ):
            z_copy(m, i).start()
        for j in range(2):
            zr[m][z, j] = zs[m, z, j]

    def kv_ready(m):
        for i in (1, 2):
            @pl.when(sp >= i)
            def _():
                kv_copy(m, i).wait_recv()

            @pl.when(sp < i)
            def _():
                (kv, vv)[m][2 - i] = jnp.zeros((ROWS, HS), BF16)

    loads[0].wait()
    loads[1].wait()
    kv_ready(0)
    end0 = plen[0, 0]
    end1 = end0 + plen[0, 1]
    keys = kv[...].reshape(3 * ROWS, HS)
    for h in range(2):
        qpos = sp * ROWS + h * HALF + lax.broadcasted_iota(jnp.int32, (HALF, 3 * ROWS), 0)
        kpos = (sp - 2) * ROWS + lax.broadcasted_iota(jnp.int32, (HALF, 3 * ROWS), 1)
        first = jnp.where(qpos >= end1, end1, jnp.where(qpos >= end0, end0, 0))
        allowed = (kpos <= qpos) & (kpos >= first)
        for n in range(0, HEADS, STACK):
            qh = jnp.concatenate(
                [qv[h * HALF:(h + 1) * HALF, m * HS:(m + 1) * HS] for m in range(n, n + STACK)], axis=0
            )
            s = lax.dot_general(qh, keys, (((1,), (1,)), ((), ())), preferred_element_type=F32)
            s = jnp.where(
                allowed[None], s.reshape(STACK, HALF, 3 * ROWS) * HS ** -0.5, big_negative
            )
            p = jnp.exp(s - jnp.max(s, axis=2, keepdims=True))
            probs[h, n * HALF:(n + STACK) * HALF] = p.astype(BF16).reshape(STACK * HALF, 3 * ROWS)
    loads[2].wait()
    kv_ready(1)
    vals = jnp.concatenate(
        [vv[...].reshape(3 * ROWS, HS), jnp.ones((3 * ROWS, HS), BF16)], axis=1
    )

    def first_copy(side):
        return copy_to(
            att.at[0, side], att.at[1, side], atts.at[side, 0], attr.at[side, 0],
            sp=(right, left)[side],
        )

    def later_copy(side, piece):
        rows = pl.ds(*PIECES[piece])
        return copy_to(
            att.at[0, 1 - side, rows], att.at[3, 1 - side, rows],
            atts.at[side, 1 + piece], attr.at[side, 1 + piece],
            sp=(right, left)[side],
        )

    def relay(side):
        return copy_to(
            att.at[1, side], att.at[2, side], atts.at[side, 3], attr.at[side, 3],
            sp=(right, left)[side],
        )

    for h in range(2):
        for n in range(0, HEADS, STACK):
            o = jnp.dot(
                probs[h, n * HALF:(n + STACK) * HALF], vals, preferred_element_type=F32
            )
            o = (o[:, :HS] / o[:, HS:]).astype(BF16)
            for m in range(STACK):
                att[0, h, :, (n + m) * HS:(n + m + 1) * HS] = o[m * HALF:(m + 1) * HALF]
        first_copy(h).start()
    for side in range(2):
        later_copy(side, 0).start()
    loads[5].wait()

    shift = 2 * core - 1
    keep_block = [sp, (sp + NSP + shift) % NSP, (sp + 2) % NSP, (sp + NSP - shift) % NSP]

    def sib_copy(k, part):
        cols = pl.ds(part * PCOLS, PCOLS)
        return copy_to(sibs.at[k, :, cols], sibr.at[k, :, cols], sbs.at[k, part], sbr.at[k, part], tp=sib)

    def product_part(k, part):
        for n in range(PCOLS // TILE):
            cols = pl.ds(part * PCOLS + n * TILE, TILE)
            v = jnp.dot(
                att[k].reshape(ROWS, FEAT), wv[:, cols], preferred_element_type=F32
            )
            keep[k, :, cols] = jnp.where(core == 0, v[:HALF], v[HALF:])
            sibs[k, :, cols] = jnp.where(core == 0, v[HALF:], v[:HALF]).astype(BF16)
        sib_copy(k, part).start()

    def product(k):
        for part in range(PARTS):
            product_part(k, part)

    def x_copy(k, part):
        cols = pl.ds(part * PCOLS, PCOLS)
        rel = (chip + NCHIP - keep_block[k] + NCHIP - 1) % NCHIP
        return copy_to(
            xs.at[k, :, cols], xr.at[rel, :, cols], xss.at[k, part], xrs.at[rel, part],
            tp=2 * keep_block[k] + core,
        )

    def x_part(k, part):
        cols = pl.ds(part * PCOLS, PCOLS)
        sib_copy(k, part).wait_recv()
        total = keep[k, :, cols] + sibr[k, :, cols].astype(F32)

        @pl.when(keep_block[k] == chip)
        def _():
            fin[:, cols] = total

        @pl.when(keep_block[k] != chip)
        def _():
            xs[k, :, cols] = total.astype(BF16)
            x_copy(k, part).start()

    def x_phase(k):
        for part in range(PARTS):
            x_part(k, part)

    far = (sp + 2) % NSP
    place = (chip + NCHIP - far) % NCHIP

    def tree_copy(part):
        cols = pl.ds(part * PCOLS, PCOLS)
        side = part // (PARTS // 2)
        to = (far + (1, NCHIP - 1)[side]) % NCHIP
        return copy_to(
            xs.at[2, :, cols], hop.at[part % (PARTS // 2)], txs.at[part], txr.at[part % (PARTS // 2)],
            tp=2 * to + core,
        )

    def far_phase():
        k = 2
        for part in range(PARTS):
            cols = pl.ds(part * PCOLS, PCOLS)
            side = part // (PARTS // 2)
            sib_copy(k, part).wait_recv()
            total = keep[k, :, cols] + sibr[k, :, cols].astype(F32)

            @pl.when(place == 0)
            def _():
                fin[:, cols] = total

            @pl.when(place == 2)
            def _():
                xs[k, :, cols] = total.astype(BF16)
                tree_copy(part).start()

            @pl.when(place == (3, 1)[side])
            def _():
                xs[k, :, cols] = total.astype(BF16)
                x_copy(k, part).start()

            @pl.when(place == (1, 3)[side])
            def _():
                keep[k, :, cols] = total

        for part in range(PARTS):
            cols = pl.ds(part * PCOLS, PCOLS)
            side = part // (PARTS // 2)

            @pl.when(place == (1, 3)[side])
            def _():
                tree_copy(part).wait_recv()
                total = keep[k, :, cols] + hop[part % (PARTS // 2)].astype(F32)
                xs[k, :, cols] = total.astype(BF16)
                x_copy(k, part).start()

        @pl.when(place == 0)
        def _():
            xr[1] = jnp.zeros((HALF, COLS), BF16)

    lane = lax.broadcasted_iota(jnp.int32, (HALF, 2 * RANK), 1)
    row = lax.broadcasted_iota(jnp.int32, (HALF, 2 * RANK), 0)
    features = pl.ds(pl.multiple_of(sp * SLICE, SLICE), SLICE)
    blocks_of = [(sp, sp), (left, right), (far, far), (right, left)]

    def low_copy(k, h):
        to = 2 * blocks_of[k][h] + h
        rel = (tp + NTP - to + NTP - 1) % NTP
        return copy_to(lxs.at[k, h], lxr.at[rel], lxss.at[k, h], lxrs.at[rel], tp=to)

    def low_rank(k):
        for h in range(2):
            sb = blocks_of[k][h]
            pair = down[pl.ds(sb, 2)].reshape(2 * RANK, SLICE)
            lr = lax.dot_general(
                att[k, h, :, features], pair, (((1,), (1,)), ((), ())), preferred_element_type=F32
            )
            early = (row + h * HALF < BLOCK - (ROWS - BLOCK) * sb).astype(jnp.int32)
            firsts = (lane < RANK).astype(jnp.int32)
            lr = jnp.where(early == firsts, lr, 0.0)

            @pl.when(2 * sb + h == tp)
            def _():
                lrs[...] = lr

            @pl.when(2 * sb + h != tp)
            def _():
                lxs[k, h] = lr.astype(BF16)
                low_copy(k, h).start()

    def cross_copy(m):
        return copy_to(cross.at[m], crossr.at[m], crs.at[m], crr.at[m], grp=other)

    def cross_send(m):
        for i in range(1, NZ):
            z_copy(m, i).wait_recv()

        def fill(b, carry):
            owner = slot_of(other, b) // SLOTS
            cross[m, b] = zr[m][owner % NZ, 1 - y_lo]
            return carry

        lax.fori_loop(0, BLOCKS, fill, 0)
        cross_copy(m).start()

    def cross_take(m, dst):
        cross_copy(m).wait_recv()

        def fill(b, carry):
            owner = slot_of(grp, b) // SLOTS
            dst[b] = jnp.where(owner // NZ == y_lo, zr[m][owner % NZ, y_lo], crossr[m, b])
            return carry

        lax.fori_loop(0, BLOCKS, fill, 0)

    def up_copy(i):
        to = (chip + i) % NCHIP
        return copy_to(
            up2own.at[pl.ds(to, 2)], up2.at[tp], ups.at[i - 1], upr.at[i - 1], tp=2 * to + core
        )

    def up_share(i):
        at = 2 * ((chip + NCHIP - i) % NCHIP) + core
        return copy_to(
            up2.at[at], up2.at[at], ups.at[NCHIP - 1 + i], upr.at[NCHIP - 1 + i], tp=sib
        )

    product(0)

    for side in range(2):
        first_copy(side).wait_recv()
        relay(side).start()
    for side in range(2):
        later_copy(side, 1).start()
    x_phase(0)
    product(1)
    cross_send(0)
    x_phase(1)

    for side in range(2):
        relay(side).wait_recv()
    product(2)
    cross_take(0, down)
    for k in range(3):
        low_rank(k)
    far_phase()

    for side in range(2):
        for piece in range(2):
            later_copy(side, piece).wait_recv()
    cross_send(1)
    low_rank(3)
    for part in range(PARTS):
        product_part(3, part)
        if part > 0:
            x_part(3, part - 1)
    x_part(3, PARTS - 1)
    cross_take(1, up2own)
    for i in range(1, NCHIP):
        up_copy(i).start()
    up2[tp] = up2own[pl.ds(chip, 2)]
    up_share(0).start()

    for rel in range(NTP - 1):
        copy_to(lxs.at[0, 0], lxr.at[rel], lxss.at[0, 0], lxrs.at[rel], tp=sib).wait_recv()
    low = lrs[...]
    for rel in range(NTP - 1):
        low = low + lxr[rel].astype(F32)
    lrs[...] = low

    def ly_copy(i):
        return copy_to(lrs, lrr.at[i - 1], lys.at[i - 1], lyr.at[i - 1], sp=(sp + i) % NSP)

    for i in range(1, NSP):
        ly_copy(i).start()
    for i in range(1, NCHIP):
        up_copy(i).wait_recv()
        up_share(i).start()
    for i in range(1, NSP):
        ly_copy(i).wait_recv()
    low = (lrs[...] + (lrr[0] + lrr[1] + lrr[2])).astype(BF16)
    for i in range(NCHIP):
        up_share(i).wait_recv()
    for part in range(PARTS):
        cols = pl.ds(part * PCOLS, PCOLS)
        for rel in range(NCHIP - 1):
            came = copy_to(
                xs.at[0, :, cols], xr.at[rel, :, cols], xss.at[0, part], xrs.at[rel, part], tp=sib
            )
            if rel == 1:
                @pl.when(place != 0)
                def _():
                    came.wait_recv()
            else:
                came.wait_recv()
        for n in range(PCOLS // SLICE):
            j = part * (PCOLS // SLICE) + n
            c = pl.ds(j * SLICE, SLICE)
            delta = jnp.dot(low, up2[j].reshape(2 * RANK, SLICE), preferred_element_type=F32)
            base = fin[:, c] + (
                xr[0, :, c].astype(F32) + xr[1, :, c].astype(F32) + xr[2, :, c].astype(F32)
            )
            out_ref[:, c] = (base + adapter_scale * delta).astype(BF16)

    for m in range(2):
        for i in (1, 2):
            @pl.when(sp + i < NSP)
            def _():
                kv_copy(m, i).wait_send()
        for i in range(1, NZ):
            z_copy(m, i).wait_send()
        cross_copy(m).wait_send()
    for side in range(2):
        first_copy(side).wait_send()
        relay(side).wait_send()
        for piece in range(2):
            later_copy(side, piece).wait_send()
    for i in range(1, NCHIP):
        up_copy(i).wait_send()
    for i in range(NCHIP):
        up_share(i).wait_send()
    for k in range(4):
        for part in range(PARTS):
            sib_copy(k, part).wait_send()

        if k == 2:
            @pl.when(place == 2)
            def _():
                for part in range(PARTS):
                    tree_copy(part).wait_send()

            @pl.when(place % 2 == 1)
            def _():
                for part in range(PARTS):
                    x_copy(k, part).wait_send()
        else:
            @pl.when(keep_block[k] != chip)
            def _():
                for part in range(PARTS):
                    x_copy(k, part).wait_send()

        for h in range(2):
            @pl.when(2 * blocks_of[k][h] + h != tp)
            def _():
                low_copy(k, h).wait_send()
    for i in range(1, NSP):
        ly_copy(i).wait_send()


def on_device(q, k, v, plen, w, dn, up, tas, tpb):
    smem = pl.BlockSpec(memory_space=pltpu.SMEM)
    anym = pl.BlockSpec(memory_space=pl.ANY)
    V = pltpu.VMEM
    D = pltpu.SemaphoreType.DMA
    return pl.pallas_call(
        kernel,
        out_shape=jax.ShapeDtypeStruct((HALF, COLS), BF16),
        in_specs=[smem] * 3 + [anym] * 6,
        out_specs=pl.BlockSpec(memory_space=pltpu.VMEM),
        scratch_shapes=[
            V((ROWS, FEAT), BF16),
            V((3, ROWS, HS), BF16),
            V((3, ROWS, HS), BF16),
            V((FEAT, COLS), BF16),
            V((SLOTS, RANK, SLICE), BF16),
            V((SLOTS, RANK, SLICE), BF16),
            V((2, HEADS * HALF, 3 * ROWS), BF16),
            V((4, 2, HALF, FEAT), BF16),
            V((4, HALF, COLS), F32),
            V((4, HALF, COLS), BF16),
            V((4, HALF, COLS), BF16),
            V((4, HALF, COLS), BF16),
            V((NCHIP - 1, HALF, COLS), BF16),
            V((PARTS // 2, HALF, PCOLS), BF16),
            V((HALF, COLS), F32),
            V((2, NZ, 2, RANK, SLICE), BF16),
            V((NZ, 2, RANK, SLICE), BF16),
            V((NZ, 2, RANK, SLICE), BF16),
            V((2, BLOCKS, RANK, SLICE), BF16),
            V((2, BLOCKS, RANK, SLICE), BF16),
            V((BLOCKS, RANK, SLICE), BF16),
            V((BLOCKS, RANK, SLICE), BF16),
            V((NTP, 2, RANK, SLICE), BF16),
            V((4, 2, HALF, 2 * RANK), BF16),
            V((NTP - 1, HALF, 2 * RANK), BF16),
            V((HALF, 2 * RANK), F32),
            V((NSP - 1, HALF, 2 * RANK), F32),
            D((6,)),
            D((2, 2)), D((2, 2)),
            D((2, 4)), D((2, 4)),
            D((2, NZ - 1)), D((2, NZ - 1)),
            D((2,)), D((2,)),
            D((2 * NCHIP - 1,)), D((2 * NCHIP - 1,)),
            D((4, PARTS)), D((4, PARTS)),
            D((4, PARTS)), D((NCHIP - 1, PARTS)),
            D((PARTS,)), D((PARTS // 2,)),
            D((4, 2)), D((NTP - 1,)),
            D((NSP - 1,)), D((NSP - 1,)),
        ],
        compiler_params=pltpu.CompilerParams(
            collective_id=0, has_side_effects=True, vmem_limit_bytes=56 * 1024 * 1024
        ),
    )(tas, tpb.T, plen, q, k, v, w, dn, up)


def solution(mesh):
    return jax.shard_map(
        on_device,
        mesh=mesh,
        in_specs=(
            P(("grp", "sp"), "tp"),
            P(("grp", "sp"), "tp"),
            P(("grp", "sp"), "tp"),
            P("grp", None),
            P("tp", "sp"),
            P("grp", None, ("tp", "sp")),
            P("grp", None, ("sp", "tp")),
            P(),
            P(),
        ),
        out_specs=P(("grp", "tp"), "sp"),
        check_vma=False,
    )
```

```python
import functools

import jax
import jax.numpy as jnp
from jax import lax
from jax.experimental import pallas as pl
from jax.experimental.pallas import tpu as pltpu
from jax.sharding import PartitionSpec as P

HS = 128
RANK = 64
BLOCK = 128
BLOCKS = 5
NSP = 4
NTP = 8
NCHIP = 4
NZ = 8
SLOTS = 4
HEADS = 8
ROWS = 160
HALF = 80
FEAT = 1024
COLS = 2048
SLICE = 256
PARTS = 4
PCOLS = COLS // PARTS
TILE = 256
STACK = 8
PIECES = ((0, 32), (32, 48))

adapter_scale = 0.5
big_negative = -1e30
MESH = pl.DeviceIdType.MESH
F32 = jnp.float32
BF16 = jnp.bfloat16


def copy_to(src, dst, ssem, rsem, **axis):
    return pltpu.make_async_remote_copy(
        src_ref=src, dst_ref=dst, send_sem=ssem, recv_sem=rsem, device_id=axis, device_id_type=MESH
    )


def kernel(
    tas, tpb, plen, q_hbm, k_hbm, v_hbm, w_hbm, dn_hbm, up_hbm, out_ref,
    qv, kv, vv, wv, dnv, upv, probs, att, keep, sibs, sibr, xs, xr, hop, fin,
    zs, zr0, zr1, cross, crossr, down, up2own, up2, lxs, lxr, lrs, lrr,
    lsem, kvs, kvr, atts, attr, zss, zrs, crs, crr, ups, upr,
    sbs, sbr, xss, xrs, txs, txr, lxss, lxrs, lys, lyr, z_in,
):
    sp = lax.axis_index("sp")
    tp = lax.axis_index("tp")
    grp = lax.axis_index("grp")
    chip = tp // 2
    core = tp % 2
    sib = tp + 1 - 2 * core
    y_lo = grp // NZ
    z = grp % NZ
    other = (1 - y_lo) * NZ + z
    zr = (zr0, zr1)
    right = (sp + 1) % NSP
    left = (sp + NSP - 1) % NSP

    loads = [
        pltpu.make_async_copy(k_hbm, kv.at[2], lsem.at[0]),
        pltpu.make_async_copy(q_hbm, qv, lsem.at[1]),
        pltpu.make_async_copy(v_hbm, vv.at[2], lsem.at[2]),
        pltpu.make_async_copy(dn_hbm, dnv, lsem.at[3]),
        pltpu.make_async_copy(up_hbm, upv, lsem.at[4]),
        pltpu.make_async_copy(w_hbm, wv, lsem.at[5]),
    ]
    barrier = pltpu.get_barrier_semaphore()
    for i in range(1, NSP):
        pl.semaphore_signal(barrier, inc=1, device_id={"sp": (sp + i) % NSP}, device_id_type=MESH)
    for i in range(1, NTP):
        pl.semaphore_signal(barrier, inc=1, device_id={"tp": (tp + i) % NTP}, device_id_type=MESH)
    pl.semaphore_signal(barrier, inc=1, device_id={"grp": other}, device_id_type=MESH)
    for i in range(1, NZ):
        @pl.when(z + i < NZ)
        def _():
            pl.semaphore_signal(barrier, inc=1, device_id={"grp": grp + i}, device_id_type=MESH)

    for c in loads:
        c.start()
    pl.semaphore_wait(barrier, (NSP - 1) + (NTP - 1) + 1 + z)
    for i in range(1, NZ):
        @pl.when(z >= i)
        def _():
            pl.semaphore_signal(z_in, inc=1, device_id={"grp": grp - i}, device_id_type=MESH)


    def kv_copy(m, i):
        return copy_to(
            (k_hbm, v_hbm)[m], (kv, vv)[m].at[2 - i], kvs.at[m, i - 1], kvr.at[m, i - 1],
            sp=(sp + i) % NSP,
        )

    for m in range(2):
        for i in (1, 2):
            @pl.when(sp + i < NSP)
            def _():
                kv_copy(m, i).start()

    loads[3].wait()
    loads[4].wait()

    def slot_of(g, b):
        return tas[tpb[b, g]]

    def pack(g, carry):
        pick = jnp.int32(0)
        for b in range(BLOCKS):
            slot = slot_of(g, b)
            pick = pick + jnp.where(slot // SLOTS == grp, slot % SLOTS, 0)
        zs[0, g % NZ, g // NZ] = dnv[pick]
        zs[1, g % NZ, g // NZ] = upv[pick]
        return carry

    lax.fori_loop(0, 2 * NZ, pack, 0)

    def z_copy(m, i):
        to = (z + i) % NZ
        return copy_to(
            zs.at[m, to], zr[m].at[z], zss.at[m, i - 1], zrs.at[m, i - 1], grp=y_lo * NZ + to
        )

    for m in range(2):
        for i in range(1, NZ):
            @pl.when(z + i >= NZ)
            def _():
                z_copy(m, i).start()

        for j in range(2):
            zr[m][z, j] = zs[m, z, j]

    def kv_ready(m):
        for i in (1, 2):
            @pl.when(sp >= i)
            def _():
                kv_copy(m, i).wait_recv()

            @pl.when(sp < i)
            def _():
                (kv, vv)[m][2 - i] = jnp.zeros((ROWS, HS), BF16)

    loads[0].wait()
    loads[1].wait()
    kv_ready(0)
    end0 = plen[0, 0]
    end1 = end0 + plen[0, 1]
    keys = kv[...].reshape(3 * ROWS, HS)
    for h in range(2):
        qpos = sp * ROWS + h * HALF + lax.broadcasted_iota(jnp.int32, (HALF, 3 * ROWS), 0)
        kpos = (sp - 2) * ROWS + lax.broadcasted_iota(jnp.int32, (HALF, 3 * ROWS), 1)
        first = jnp.where(qpos >= end1, end1, jnp.where(qpos >= end0, end0, 0))
        allowed = (kpos <= qpos) & (kpos >= first)
        for n in range(0, HEADS, STACK):
            qh = jnp.concatenate(
                [qv[h * HALF:(h + 1) * HALF, m * HS:(m + 1) * HS] for m in range(n, n + STACK)], axis=0
            )
            s = lax.dot_general(qh, keys, (((1,), (1,)), ((), ())), preferred_element_type=F32)
            s = jnp.where(
                allowed[None], s.reshape(STACK, HALF, 3 * ROWS) * HS ** -0.5, big_negative
            )
            p = jnp.exp(s - jnp.max(s, axis=2, keepdims=True))
            probs[h, n * HALF:(n + STACK) * HALF] = p.astype(BF16).reshape(STACK * HALF, 3 * ROWS)
    loads[2].wait()
    kv_ready(1)
    vals = jnp.concatenate(
        [vv[...].reshape(3 * ROWS, HS), jnp.ones((3 * ROWS, HS), BF16)], axis=1
    )

    def first_copy(side):
        return copy_to(
            att.at[0, side], att.at[1, side], atts.at[side, 0], attr.at[side, 0],
            sp=(right, left)[side],
        )

    def later_copy(side, piece):
        rows = pl.ds(*PIECES[piece])
        return copy_to(
            att.at[0, 1 - side, rows], att.at[3, 1 - side, rows],
            atts.at[side, 1 + piece], attr.at[side, 1 + piece],
            sp=(right, left)[side],
        )

    def relay(side):
        return copy_to(
            att.at[1, side], att.at[2, side], atts.at[side, 3], attr.at[side, 3],
            sp=(right, left)[side],
        )

    for h in range(2):
        for n in range(0, HEADS, STACK):
            o = jnp.dot(
                probs[h, n * HALF:(n + STACK) * HALF], vals, preferred_element_type=F32
            )
            o = (o[:, :HS] / o[:, HS:]).astype(BF16)
            for m in range(STACK):
                att[0, h, :, (n + m) * HS:(n + m + 1) * HS] = o[m * HALF:(m + 1) * HALF]
        first_copy(h).start()
    for side in range(2):
        later_copy(side, 0).start()

    @pl.when(z < NZ - 1)
    def _():
        pl.semaphore_wait(z_in, NZ - 1 - z)

    for m in range(2):
        for i in range(1, NZ):
            @pl.when(z + i < NZ)
            def _():
                z_copy(m, i).start()

    loads[5].wait()

    shift = 2 * core - 1
    keep_block = [sp, (sp + NSP + shift) % NSP, (sp + 2) % NSP, (sp + NSP - shift) % NSP]

    def sib_copy(k, part):
        cols = pl.ds(part * PCOLS, PCOLS)
        return copy_to(sibs.at[k, :, cols], sibr.at[k, :, cols], sbs.at[k, part], sbr.at[k, part], tp=sib)

    def product_part(k, part):
        for n in range(PCOLS // TILE):
            cols = pl.ds(part * PCOLS + n * TILE, TILE)
            v = jnp.dot(
                att[k].reshape(ROWS, FEAT), wv[:, cols], preferred_element_type=F32
            )
            keep[k, :, cols] = jnp.where(core == 0, v[:HALF], v[HALF:])
            sibs[k, :, cols] = jnp.where(core == 0, v[HALF:], v[:HALF]).astype(BF16)
        sib_copy(k, part).start()

    def product(k):
        for part in range(PARTS):
            product_part(k, part)

    def x_copy(k, part):
        cols = pl.ds(part * PCOLS, PCOLS)
        rel = (chip + NCHIP - keep_block[k] + NCHIP - 1) % NCHIP
        return copy_to(
            xs.at[k, :, cols], xr.at[rel, :, cols], xss.at[k, part], xrs.at[rel, part],
            tp=2 * keep_block[k] + core,
        )

    def x_part(k, part):
        cols = pl.ds(part * PCOLS, PCOLS)
        sib_copy(k, part).wait_recv()
        total = keep[k, :, cols] + sibr[k, :, cols].astype(F32)

        @pl.when(keep_block[k] == chip)
        def _():
            fin[:, cols] = total

        @pl.when(keep_block[k] != chip)
        def _():
            xs[k, :, cols] = total.astype(BF16)
            x_copy(k, part).start()

    def x_phase(k):
        for part in range(PARTS):
            x_part(k, part)

    far = (sp + 2) % NSP
    place = (chip + NCHIP - far) % NCHIP

    def tree_copy(part):
        cols = pl.ds(part * PCOLS, PCOLS)
        side = part // (PARTS // 2)
        to = (far + (1, NCHIP - 1)[side]) % NCHIP
        return copy_to(
            xs.at[2, :, cols], hop.at[part % (PARTS // 2)], txs.at[part], txr.at[part % (PARTS // 2)],
            tp=2 * to + core,
        )

    def far_phase():
        k = 2
        for part in range(PARTS):
            cols = pl.ds(part * PCOLS, PCOLS)
            side = part // (PARTS // 2)
            sib_copy(k, part).wait_recv()
            total = keep[k, :, cols] + sibr[k, :, cols].astype(F32)

            @pl.when(place == 0)
            def _():
                fin[:, cols] = total

            @pl.when(place == 2)
            def _():
                xs[k, :, cols] = total.astype(BF16)
                tree_copy(part).start()

            @pl.when(place == (3, 1)[side])
            def _():
                xs[k, :, cols] = total.astype(BF16)
                x_copy(k, part).start()

            @pl.when(place == (1, 3)[side])
            def _():
                keep[k, :, cols] = total

        for part in range(PARTS):
            cols = pl.ds(part * PCOLS, PCOLS)
            side = part // (PARTS // 2)

            @pl.when(place == (1, 3)[side])
            def _():
                tree_copy(part).wait_recv()
                total = keep[k, :, cols] + hop[part % (PARTS // 2)].astype(F32)
                xs[k, :, cols] = total.astype(BF16)
                x_copy(k, part).start()

        @pl.when(place == 0)
        def _():
            xr[1] = jnp.zeros((HALF, COLS), BF16)

    lane = lax.broadcasted_iota(jnp.int32, (HALF, 2 * RANK), 1)
    row = lax.broadcasted_iota(jnp.int32, (HALF, 2 * RANK), 0)
    features = pl.ds(pl.multiple_of(sp * SLICE, SLICE), SLICE)
    blocks_of = [(sp, sp), (left, right), (far, far), (right, left)]

    def low_copy(k, h):
        to = 2 * blocks_of[k][h] + h
        rel = (tp + NTP - to + NTP - 1) % NTP
        return copy_to(lxs.at[k, h], lxr.at[rel], lxss.at[k, h], lxrs.at[rel], tp=to)

    def low_rank(k):
        for h in range(2):
            sb = blocks_of[k][h]
            pair = down[pl.ds(sb, 2)].reshape(2 * RANK, SLICE)
            lr = lax.dot_general(
                att[k, h, :, features], pair, (((1,), (1,)), ((), ())), preferred_element_type=F32
            )
            early = (row + h * HALF < BLOCK - (ROWS - BLOCK) * sb).astype(jnp.int32)
            firsts = (lane < RANK).astype(jnp.int32)
            lr = jnp.where(early == firsts, lr, 0.0)

            @pl.when(2 * sb + h == tp)
            def _():
                lrs[...] = lr

            @pl.when(2 * sb + h != tp)
            def _():
                lxs[k, h] = lr.astype(BF16)
                low_copy(k, h).start()

    def cross_copy(m):
        return copy_to(cross.at[m], crossr.at[m], crs.at[m], crr.at[m], grp=other)

    def cross_send(m):
        for i in range(1, NZ):
            z_copy(m, i).wait_recv()

        def fill(b, carry):
            owner = slot_of(other, b) // SLOTS
            cross[m, b] = zr[m][owner % NZ, 1 - y_lo]
            return carry

        lax.fori_loop(0, BLOCKS, fill, 0)
        cross_copy(m).start()

    def cross_take(m, dst):
        cross_copy(m).wait_recv()

        def fill(b, carry):
            owner = slot_of(grp, b) // SLOTS
            dst[b] = jnp.where(owner // NZ == y_lo, zr[m][owner % NZ, y_lo], crossr[m, b])
            return carry

        lax.fori_loop(0, BLOCKS, fill, 0)

    def up_copy(i):
        to = (chip + i) % NCHIP
        return copy_to(
            up2own.at[pl.ds(to, 2)], up2.at[tp], ups.at[i - 1], upr.at[i - 1], tp=2 * to + core
        )

    def up_share(i):
        at = 2 * ((chip + NCHIP - i) % NCHIP) + core
        return copy_to(
            up2.at[at], up2.at[at], ups.at[NCHIP - 1 + i], upr.at[NCHIP - 1 + i], tp=sib
        )

    product(0)

    for side in range(2):
        first_copy(side).wait_recv()
        relay(side).start()
    for side in range(2):
        later_copy(side, 1).start()
    x_phase(0)
    product(1)
    x_phase(1)

    for side in range(2):
        relay(side).wait_recv()
    product(2)
    far_phase()

    for side in range(2):
        for piece in range(2):
            later_copy(side, piece).wait_recv()
    cross_send(0)
    cross_send(1)
    for part in range(PARTS):
        product_part(3, part)
        if part > 0:
            x_part(3, part - 1)
    x_part(3, PARTS - 1)
    cross_take(0, down)
    for k in range(4):
        low_rank(k)
    cross_take(1, up2own)
    for i in range(1, NCHIP):
        up_copy(i).start()
    up2[tp] = up2own[pl.ds(chip, 2)]
    up_share(0).start()

    for rel in range(NTP - 1):
        copy_to(lxs.at[0, 0], lxr.at[rel], lxss.at[0, 0], lxrs.at[rel], tp=sib).wait_recv()
    low = lrs[...]
    for rel in range(NTP - 1):
        low = low + lxr[rel].astype(F32)
    lrs[...] = low

    def ly_copy(i):
        return copy_to(lrs, lrr.at[i - 1], lys.at[i - 1], lyr.at[i - 1], sp=(sp + i) % NSP)

    for i in range(1, NSP):
        ly_copy(i).start()
    for i in range(1, NCHIP):
        up_copy(i).wait_recv()
        up_share(i).start()
    for i in range(1, NSP):
        ly_copy(i).wait_recv()
    low = (lrs[...] + (lrr[0] + lrr[1] + lrr[2])).astype(BF16)
    for i in range(NCHIP):
        up_share(i).wait_recv()
    for part in range(PARTS):
        cols = pl.ds(part * PCOLS, PCOLS)
        for rel in range(NCHIP - 1):
            came = copy_to(
                xs.at[0, :, cols], xr.at[rel, :, cols], xss.at[0, part], xrs.at[rel, part], tp=sib
            )
            if rel == 1:
                @pl.when(place != 0)
                def _():
                    came.wait_recv()
            else:
                came.wait_recv()
        for n in range(PCOLS // SLICE):
            j = part * (PCOLS // SLICE) + n
            c = pl.ds(j * SLICE, SLICE)
            delta = jnp.dot(low, up2[j].reshape(2 * RANK, SLICE), preferred_element_type=F32)
            base = fin[:, c] + (
                xr[0, :, c].astype(F32) + xr[1, :, c].astype(F32) + xr[2, :, c].astype(F32)
            )
            out_ref[:, c] = (base + adapter_scale * delta).astype(BF16)

    for m in range(2):
        for i in (1, 2):
            @pl.when(sp + i < NSP)
            def _():
                kv_copy(m, i).wait_send()
        for i in range(1, NZ):
            z_copy(m, i).wait_send()
        cross_copy(m).wait_send()
    for side in range(2):
        first_copy(side).wait_send()
        relay(side).wait_send()
        for piece in range(2):
            later_copy(side, piece).wait_send()
    for i in range(1, NCHIP):
        up_copy(i).wait_send()
    for i in range(NCHIP):
        up_share(i).wait_send()
    for k in range(4):
        for part in range(PARTS):
            sib_copy(k, part).wait_send()

        if k == 2:
            @pl.when(place == 2)
            def _():
                for part in range(PARTS):
                    tree_copy(part).wait_send()

            @pl.when(place % 2 == 1)
            def _():
                for part in range(PARTS):
                    x_copy(k, part).wait_send()
        else:
            @pl.when(keep_block[k] != chip)
            def _():
                for part in range(PARTS):
                    x_copy(k, part).wait_send()

        for h in range(2):
            @pl.when(2 * blocks_of[k][h] + h != tp)
            def _():
                low_copy(k, h).wait_send()
    for i in range(1, NSP):
        ly_copy(i).wait_send()


def on_device(q, k, v, plen, w, dn, up, tas, tpb):
    smem = pl.BlockSpec(memory_space=pltpu.SMEM)
    anym = pl.BlockSpec(memory_space=pl.ANY)
    V = pltpu.VMEM
    D = pltpu.SemaphoreType.DMA
    return pl.pallas_call(
        kernel,
        out_shape=jax.ShapeDtypeStruct((HALF, COLS), BF16),
        in_specs=[smem] * 3 + [anym] * 6,
        out_specs=pl.BlockSpec(memory_space=pltpu.VMEM),
        scratch_shapes=[
            V((ROWS, FEAT), BF16),
            V((3, ROWS, HS), BF16),
            V((3, ROWS, HS), BF16),
            V((FEAT, COLS), BF16),
            V((SLOTS, RANK, SLICE), BF16),
            V((SLOTS, RANK, SLICE), BF16),
            V((2, HEADS * HALF, 3 * ROWS), BF16),
            V((4, 2, HALF, FEAT), BF16),
            V((4, HALF, COLS), F32),
            V((4, HALF, COLS), BF16),
            V((4, HALF, COLS), BF16),
            V((4, HALF, COLS), BF16),
            V((NCHIP - 1, HALF, COLS), BF16),
            V((PARTS // 2, HALF, PCOLS), BF16),
            V((HALF, COLS), F32),
            V((2, NZ, 2, RANK, SLICE), BF16),
            V((NZ, 2, RANK, SLICE), BF16),
            V((NZ, 2, RANK, SLICE), BF16),
            V((2, BLOCKS, RANK, SLICE), BF16),
            V((2, BLOCKS, RANK, SLICE), BF16),
            V((BLOCKS, RANK, SLICE), BF16),
            V((BLOCKS, RANK, SLICE), BF16),
            V((NTP, 2, RANK, SLICE), BF16),
            V((4, 2, HALF, 2 * RANK), BF16),
            V((NTP - 1, HALF, 2 * RANK), BF16),
            V((HALF, 2 * RANK), F32),
            V((NSP - 1, HALF, 2 * RANK), F32),
            D((6,)),
            D((2, 2)), D((2, 2)),
            D((2, 4)), D((2, 4)),
            D((2, NZ - 1)), D((2, NZ - 1)),
            D((2,)), D((2,)),
            D((2 * NCHIP - 1,)), D((2 * NCHIP - 1,)),
            D((4, PARTS)), D((4, PARTS)),
            D((4, PARTS)), D((NCHIP - 1, PARTS)),
            D((PARTS,)), D((PARTS // 2,)),
            D((4, 2)), D((NTP - 1,)),
            D((NSP - 1,)), D((NSP - 1,)),
            pltpu.SemaphoreType.REGULAR,
        ],
        compiler_params=pltpu.CompilerParams(
            collective_id=0, has_side_effects=True, vmem_limit_bytes=56 * 1024 * 1024
        ),
    )(tas, tpb.T, plen, q, k, v, w, dn, up)


def solution(mesh):
    return jax.shard_map(
        on_device,
        mesh=mesh,
        in_specs=(
            P(("grp", "sp"), "tp"),
            P(("grp", "sp"), "tp"),
            P(("grp", "sp"), "tp"),
            P("grp", None),
            P("tp", "sp"),
            P("grp", None, ("tp", "sp")),
            P("grp", None, ("sp", "tp")),
            P(),
            P(),
        ),
        out_specs=P(("grp", "tp"), "sp"),
        check_vma=False,
    )
```

```python
import functools

import jax
import jax.numpy as jnp
from jax import lax
from jax.experimental import pallas as pl
from jax.experimental.pallas import tpu as pltpu
from jax.sharding import PartitionSpec as P

HS = 128
RANK = 64
BLOCK = 128
BLOCKS = 5
NSP = 4
NTP = 8
NCHIP = 4
NZ = 8
SLOTS = 4
HEADS = 8
ROWS = 160
HALF = 80
FEAT = 1024
COLS = 2048
SLICE = 256
PARTS = 4
PCOLS = COLS // PARTS
TILE = 256
STACK = 8
PIECES = ((0, 32), (32, 48))

adapter_scale = 0.5
big_negative = -1e30
MESH = pl.DeviceIdType.MESH
F32 = jnp.float32
BF16 = jnp.bfloat16


def copy_to(src, dst, ssem, rsem, **axis):
    return pltpu.make_async_remote_copy(
        src_ref=src, dst_ref=dst, send_sem=ssem, recv_sem=rsem, device_id=axis, device_id_type=MESH
    )


def kernel(
    tas, tpb, plen, q_hbm, k_hbm, v_hbm, w_hbm, dn_hbm, up_hbm, out_ref,
    qv, kv, vv, wv, dnv, upv, probs, att, keep, sibs, sibr, xs, xr, hop, fin,
    zs, zr0, zr1, cross, crossr, down, up2own, up2, lxs, lxr, lrs, lyx, lrr,
    lsem, kvs, kvr, atts, attr, zss, zrs, crs, crr, ups, upr,
    sbs, sbr, xss, xrs, txs, txr, lxss, lxrs, lys, lyr, z_in,
):
    sp = lax.axis_index("sp")
    tp = lax.axis_index("tp")
    grp = lax.axis_index("grp")
    chip = tp // 2
    core = tp % 2
    sib = tp + 1 - 2 * core
    y_lo = grp // NZ
    z = grp % NZ
    other = (1 - y_lo) * NZ + z
    zr = (zr0, zr1)
    right = (sp + 1) % NSP
    left = (sp + NSP - 1) % NSP

    loads = [
        pltpu.make_async_copy(k_hbm, kv.at[2], lsem.at[0]),
        pltpu.make_async_copy(q_hbm, qv, lsem.at[1]),
        pltpu.make_async_copy(v_hbm, vv.at[2], lsem.at[2]),
        pltpu.make_async_copy(dn_hbm, dnv, lsem.at[3]),
        pltpu.make_async_copy(up_hbm, upv, lsem.at[4]),
        pltpu.make_async_copy(w_hbm, wv, lsem.at[5]),
    ]
    barrier = pltpu.get_barrier_semaphore()
    for i in range(1, NSP):
        pl.semaphore_signal(barrier, inc=1, device_id={"sp": (sp + i) % NSP}, device_id_type=MESH)
    for i in range(1, NTP):
        pl.semaphore_signal(barrier, inc=1, device_id={"tp": (tp + i) % NTP}, device_id_type=MESH)
    pl.semaphore_signal(barrier, inc=1, device_id={"grp": other}, device_id_type=MESH)
    for i in range(1, NZ):
        @pl.when(z + i < NZ)
        def _():
            pl.semaphore_signal(barrier, inc=1, device_id={"grp": grp + i}, device_id_type=MESH)

    for c in loads:
        c.start()
    pl.semaphore_wait(barrier, (NSP - 1) + (NTP - 1) + 1 + z)
    for i in range(1, NZ):
        @pl.when(z >= i)
        def _():
            pl.semaphore_signal(z_in, inc=1, device_id={"grp": grp - i}, device_id_type=MESH)


    def kv_copy(m, i):
        return copy_to(
            (k_hbm, v_hbm)[m], (kv, vv)[m].at[2 - i], kvs.at[m, i - 1], kvr.at[m, i - 1],
            sp=(sp + i) % NSP,
        )

    for m in range(2):
        for i in (1, 2):
            @pl.when(sp + i < NSP)
            def _():
                kv_copy(m, i).start()

    loads[3].wait()
    loads[4].wait()

    def slot_of(g, b):
        return tas[tpb[b, g]]

    def pack(g, carry):
        pick = jnp.int32(0)
        for b in range(BLOCKS):
            slot = slot_of(g, b)
            pick = pick + jnp.where(slot // SLOTS == grp, slot % SLOTS, 0)
        zs[0, g % NZ, g // NZ] = dnv[pick]
        zs[1, g % NZ, g // NZ] = upv[pick]
        return carry

    lax.fori_loop(0, 2 * NZ, pack, 0)

    def z_copy(m, i):
        to = (z + i) % NZ
        return copy_to(
            zs.at[m, to], zr[m].at[z], zss.at[m, i - 1], zrs.at[m, i - 1], grp=y_lo * NZ + to
        )

    for i in range(1, NZ):
        @pl.when(z + i >= NZ)
        def _():
            z_copy(0, i).start()

    for m in range(2):
        for j in range(2):
            zr[m][z, j] = zs[m, z, j]

    def kv_ready(m):
        for i in (1, 2):
            @pl.when(sp >= i)
            def _():
                kv_copy(m, i).wait_recv()

            @pl.when(sp < i)
            def _():
                (kv, vv)[m][2 - i] = jnp.zeros((ROWS, HS), BF16)

    loads[0].wait()
    loads[1].wait()
    kv_ready(0)
    end0 = plen[0, 0]
    end1 = end0 + plen[0, 1]
    keys = kv[...].reshape(3 * ROWS, HS)
    for h in range(2):
        qpos = sp * ROWS + h * HALF + lax.broadcasted_iota(jnp.int32, (HALF, 3 * ROWS), 0)
        kpos = (sp - 2) * ROWS + lax.broadcasted_iota(jnp.int32, (HALF, 3 * ROWS), 1)
        first = jnp.where(qpos >= end1, end1, jnp.where(qpos >= end0, end0, 0))
        allowed = (kpos <= qpos) & (kpos >= first)
        for n in range(0, HEADS, STACK):
            qh = jnp.concatenate(
                [qv[h * HALF:(h + 1) * HALF, m * HS:(m + 1) * HS] for m in range(n, n + STACK)], axis=0
            )
            s = lax.dot_general(qh, keys, (((1,), (1,)), ((), ())), preferred_element_type=F32)
            s = jnp.where(
                allowed[None], s.reshape(STACK, HALF, 3 * ROWS) * HS ** -0.5, big_negative
            )
            p = jnp.exp(s - jnp.max(s, axis=2, keepdims=True))
            probs[h, n * HALF:(n + STACK) * HALF] = p.astype(BF16).reshape(STACK * HALF, 3 * ROWS)
    loads[2].wait()
    kv_ready(1)
    vals = jnp.concatenate(
        [vv[...].reshape(3 * ROWS, HS), jnp.ones((3 * ROWS, HS), BF16)], axis=1
    )

    def first_copy(side):
        return copy_to(
            att.at[0, side], att.at[1, side], atts.at[side, 0], attr.at[side, 0],
            sp=(right, left)[side],
        )

    def later_copy(side, piece):
        rows = pl.ds(*PIECES[piece])
        return copy_to(
            att.at[0, 1 - side, rows], att.at[3, 1 - side, rows],
            atts.at[side, 1 + piece], attr.at[side, 1 + piece],
            sp=(right, left)[side],
        )

    def relay(side):
        return copy_to(
            att.at[1, side], att.at[2, side], atts.at[side, 3], attr.at[side, 3],
            sp=(right, left)[side],
        )

    for h in range(2):
        for n in range(0, HEADS, STACK):
            o = jnp.dot(
                probs[h, n * HALF:(n + STACK) * HALF], vals, preferred_element_type=F32
            )
            o = (o[:, :HS] / o[:, HS:]).astype(BF16)
            for m in range(STACK):
                att[0, h, :, (n + m) * HS:(n + m + 1) * HS] = o[m * HALF:(m + 1) * HALF]
        first_copy(h).start()
    for side in range(2):
        later_copy(side, 0).start()

    @pl.when(z < NZ - 1)
    def _():
        pl.semaphore_wait(z_in, NZ - 1 - z)

    for i in range(1, NZ):
        @pl.when(z + i < NZ)
        def _():
            z_copy(0, i).start()

    loads[5].wait()

    shift = 2 * core - 1
    keep_block = [sp, (sp + NSP + shift) % NSP, (sp + 2) % NSP, (sp + NSP - shift) % NSP]

    def sib_copy(k, part):
        cols = pl.ds(part * PCOLS, PCOLS)
        return copy_to(sibs.at[k, :, cols], sibr.at[k, :, cols], sbs.at[k, part], sbr.at[k, part], tp=sib)

    def product_part(k, part):
        for n in range(PCOLS // TILE):
            cols = pl.ds(part * PCOLS + n * TILE, TILE)
            v = jnp.dot(
                att[k].reshape(ROWS, FEAT), wv[:, cols], preferred_element_type=F32
            )
            keep[k, :, cols] = jnp.where(core == 0, v[:HALF], v[HALF:])
            sibs[k, :, cols] = jnp.where(core == 0, v[HALF:], v[:HALF]).astype(BF16)
        sib_copy(k, part).start()

    def product(k):
        for part in range(PARTS):
            product_part(k, part)

    def x_copy(k, part):
        cols = pl.ds(part * PCOLS, PCOLS)
        rel = (chip + NCHIP - keep_block[k] + NCHIP - 1) % NCHIP
        return copy_to(
            xs.at[k, :, cols], xr.at[rel, :, cols], xss.at[k, part], xrs.at[rel, part],
            tp=2 * keep_block[k] + core,
        )

    def x_part(k, part):
        cols = pl.ds(part * PCOLS, PCOLS)
        sib_copy(k, part).wait_recv()
        total = keep[k, :, cols] + sibr[k, :, cols].astype(F32)

        @pl.when(keep_block[k] == chip)
        def _():
            fin[:, cols] = total

        @pl.when(keep_block[k] != chip)
        def _():
            xs[k, :, cols] = total.astype(BF16)
            x_copy(k, part).start()

    def x_phase(k):
        for part in range(PARTS):
            x_part(k, part)

    far = (sp + 2) % NSP
    place = (chip + NCHIP - far) % NCHIP

    def tree_copy(part):
        cols = pl.ds(part * PCOLS, PCOLS)
        side = part // (PARTS // 2)
        to = (far + (1, NCHIP - 1)[side]) % NCHIP
        return copy_to(
            xs.at[2, :, cols], hop.at[part % (PARTS // 2)], txs.at[part], txr.at[part % (PARTS // 2)],
            tp=2 * to + core,
        )

    def far_phase():
        k = 2
        for part in range(PARTS):
            cols = pl.ds(part * PCOLS, PCOLS)
            side = part // (PARTS // 2)
            sib_copy(k, part).wait_recv()
            total = keep[k, :, cols] + sibr[k, :, cols].astype(F32)

            @pl.when(place == 0)
            def _():
                fin[:, cols] = total

            @pl.when(place == 2)
            def _():
                xs[k, :, cols] = total.astype(BF16)
                tree_copy(part).start()

            @pl.when(place == (3, 1)[side])
            def _():
                xs[k, :, cols] = total.astype(BF16)
                x_copy(k, part).start()

            @pl.when(place == (1, 3)[side])
            def _():
                keep[k, :, cols] = total

        for part in range(PARTS):
            cols = pl.ds(part * PCOLS, PCOLS)
            side = part // (PARTS // 2)

            @pl.when(place == (1, 3)[side])
            def _():
                tree_copy(part).wait_recv()
                total = keep[k, :, cols] + hop[part % (PARTS // 2)].astype(F32)
                xs[k, :, cols] = total.astype(BF16)
                x_copy(k, part).start()

        @pl.when(place == 0)
        def _():
            xr[1] = jnp.zeros((HALF, COLS), BF16)

    lane = lax.broadcasted_iota(jnp.int32, (HALF, 2 * RANK), 1)
    row = lax.broadcasted_iota(jnp.int32, (HALF, 2 * RANK), 0)
    features = pl.ds(pl.multiple_of(sp * SLICE, SLICE), SLICE)
    blocks_of = [(sp, sp), (left, right), (far, far), (right, left)]

    def low_copy(k, h):
        to = 2 * blocks_of[k][h] + h
        rel = (tp + NTP - to + NTP - 1) % NTP
        return copy_to(lxs.at[k, h], lxr.at[rel], lxss.at[k, h], lxrs.at[rel], tp=to)

    def low_rank(k):
        for h in range(2):
            sb = blocks_of[k][h]
            pair = down[pl.ds(sb, 2)].reshape(2 * RANK, SLICE)
            lr = lax.dot_general(
                att[k, h, :, features], pair, (((1,), (1,)), ((), ())), preferred_element_type=F32
            )
            early = (row + h * HALF < BLOCK - (ROWS - BLOCK) * sb).astype(jnp.int32)
            firsts = (lane < RANK).astype(jnp.int32)
            lr = jnp.where(early == firsts, lr, 0.0)

            @pl.when(2 * sb + h == tp)
            def _():
                lrs[...] = lr

            @pl.when(2 * sb + h != tp)
            def _():
                lxs[k, h] = lr.astype(BF16)
                low_copy(k, h).start()

    def cross_copy(m):
        return copy_to(cross.at[m], crossr.at[m], crs.at[m], crr.at[m], grp=other)

    def cross_send(m):
        for i in range(1, NZ):
            z_copy(m, i).wait_recv()

        def fill(b, carry):
            owner = slot_of(other, b) // SLOTS
            cross[m, b] = zr[m][owner % NZ, 1 - y_lo]
            return carry

        lax.fori_loop(0, BLOCKS, fill, 0)
        cross_copy(m).start()

    def cross_take(m, dst):
        cross_copy(m).wait_recv()

        def fill(b, carry):
            owner = slot_of(grp, b) // SLOTS
            dst[b] = jnp.where(owner // NZ == y_lo, zr[m][owner % NZ, y_lo], crossr[m, b])
            return carry

        lax.fori_loop(0, BLOCKS, fill, 0)

    def up_copy(i):
        to = (chip + i) % NCHIP
        return copy_to(
            up2own.at[pl.ds(to, 2)], up2.at[tp], ups.at[i - 1], upr.at[i - 1], tp=2 * to + core
        )

    def up_share(i):
        at = 2 * ((chip + NCHIP - i) % NCHIP) + core
        return copy_to(
            up2.at[at], up2.at[at], ups.at[NCHIP - 1 + i], upr.at[NCHIP - 1 + i], tp=sib
        )

    product(0)

    for side in range(2):
        first_copy(side).wait_recv()
        relay(side).start()
    for side in range(2):
        later_copy(side, 1).start()
    x_phase(0)
    for i in range(1, NZ):
        z_copy(1, i).start()
    product(1)
    x_phase(1)
    cross_send(0)

    for side in range(2):
        relay(side).wait_recv()
    product(2)
    far_phase()
    cross_take(0, down)
    for k in range(3):
        low_rank(k)

    for side in range(2):
        for piece in range(2):
            later_copy(side, piece).wait_recv()
    low_rank(3)
    for part in range(PARTS):
        product_part(3, part)
        if part > 0:
            x_part(3, part - 1)
    x_part(3, PARTS - 1)

    for rel in range(NTP - 1):
        copy_to(lxs.at[0, 0], lxr.at[rel], lxss.at[0, 0], lxrs.at[rel], tp=sib).wait_recv()
    low = lrs[...]
    for rel in range(NTP - 1):
        low = low + lxr[rel].astype(F32)
    lrs[...] = low
    lyx[...] = low.astype(BF16)

    def ly_copy(i):
        return copy_to(lyx, lrr.at[i - 1], lys.at[i - 1], lyr.at[i - 1], sp=(sp + i) % NSP)

    for i in range(1, NSP):
        ly_copy(i).start()

    cross_send(1)
    cross_take(1, up2own)
    for i in range(1, NCHIP):
        up_copy(i).start()
    up2[tp] = up2own[pl.ds(chip, 2)]
    up_share(0).start()
    for i in range(1, NCHIP):
        up_copy(i).wait_recv()
        up_share(i).start()
    for i in range(1, NSP):
        ly_copy(i).wait_recv()
    low = lrs[...]
    for i in range(NSP - 1):
        low = low + lrr[i].astype(F32)
    low = low.astype(BF16)
    for i in range(NCHIP):
        up_share(i).wait_recv()
    for part in range(PARTS):
        cols = pl.ds(part * PCOLS, PCOLS)
        for rel in range(NCHIP - 1):
            came = copy_to(
                xs.at[0, :, cols], xr.at[rel, :, cols], xss.at[0, part], xrs.at[rel, part], tp=sib
            )
            if rel == 1:
                @pl.when(place != 0)
                def _():
                    came.wait_recv()
            else:
                came.wait_recv()
        for n in range(PCOLS // SLICE):
            j = part * (PCOLS // SLICE) + n
            c = pl.ds(j * SLICE, SLICE)
            delta = jnp.dot(low, up2[j].reshape(2 * RANK, SLICE), preferred_element_type=F32)
            base = fin[:, c] + (
                xr[0, :, c].astype(F32) + xr[1, :, c].astype(F32) + xr[2, :, c].astype(F32)
            )
            out_ref[:, c] = (base + adapter_scale * delta).astype(BF16)

    for m in range(2):
        for i in (1, 2):
            @pl.when(sp + i < NSP)
            def _():
                kv_copy(m, i).wait_send()
        for i in range(1, NZ):
            z_copy(m, i).wait_send()
        cross_copy(m).wait_send()
    for side in range(2):
        first_copy(side).wait_send()
        relay(side).wait_send()
        for piece in range(2):
            later_copy(side, piece).wait_send()
    for i in range(1, NCHIP):
        up_copy(i).wait_send()
    for i in range(NCHIP):
        up_share(i).wait_send()
    for k in range(4):
        for part in range(PARTS):
            sib_copy(k, part).wait_send()

        if k == 2:
            @pl.when(place == 2)
            def _():
                for part in range(PARTS):
                    tree_copy(part).wait_send()

            @pl.when(place % 2 == 1)
            def _():
                for part in range(PARTS):
                    x_copy(k, part).wait_send()
        else:
            @pl.when(keep_block[k] != chip)
            def _():
                for part in range(PARTS):
                    x_copy(k, part).wait_send()

        for h in range(2):
            @pl.when(2 * blocks_of[k][h] + h != tp)
            def _():
                low_copy(k, h).wait_send()
    for i in range(1, NSP):
        ly_copy(i).wait_send()


def on_device(q, k, v, plen, w, dn, up, tas, tpb):
    smem = pl.BlockSpec(memory_space=pltpu.SMEM)
    anym = pl.BlockSpec(memory_space=pl.ANY)
    V = pltpu.VMEM
    D = pltpu.SemaphoreType.DMA
    return pl.pallas_call(
        kernel,
        out_shape=jax.ShapeDtypeStruct((HALF, COLS), BF16),
        in_specs=[smem] * 3 + [anym] * 6,
        out_specs=pl.BlockSpec(memory_space=pltpu.VMEM),
        scratch_shapes=[
            V((ROWS, FEAT), BF16),
            V((3, ROWS, HS), BF16),
            V((3, ROWS, HS), BF16),
            V((FEAT, COLS), BF16),
            V((SLOTS, RANK, SLICE), BF16),
            V((SLOTS, RANK, SLICE), BF16),
            V((2, HEADS * HALF, 3 * ROWS), BF16),
            V((4, 2, HALF, FEAT), BF16),
            V((4, HALF, COLS), F32),
            V((4, HALF, COLS), BF16),
            V((4, HALF, COLS), BF16),
            V((4, HALF, COLS), BF16),
            V((NCHIP - 1, HALF, COLS), BF16),
            V((PARTS // 2, HALF, PCOLS), BF16),
            V((HALF, COLS), F32),
            V((2, NZ, 2, RANK, SLICE), BF16),
            V((NZ, 2, RANK, SLICE), BF16),
            V((NZ, 2, RANK, SLICE), BF16),
            V((2, BLOCKS, RANK, SLICE), BF16),
            V((2, BLOCKS, RANK, SLICE), BF16),
            V((BLOCKS, RANK, SLICE), BF16),
            V((BLOCKS, RANK, SLICE), BF16),
            V((NTP, 2, RANK, SLICE), BF16),
            V((4, 2, HALF, 2 * RANK), BF16),
            V((NTP - 1, HALF, 2 * RANK), BF16),
            V((HALF, 2 * RANK), F32),
            V((HALF, 2 * RANK), BF16),
            V((NSP - 1, HALF, 2 * RANK), BF16),
            D((6,)),
            D((2, 2)), D((2, 2)),
            D((2, 4)), D((2, 4)),
            D((2, NZ - 1)), D((2, NZ - 1)),
            D((2,)), D((2,)),
            D((2 * NCHIP - 1,)), D((2 * NCHIP - 1,)),
            D((4, PARTS)), D((4, PARTS)),
            D((4, PARTS)), D((NCHIP - 1, PARTS)),
            D((PARTS,)), D((PARTS // 2,)),
            D((4, 2)), D((NTP - 1,)),
            D((NSP - 1,)), D((NSP - 1,)),
            pltpu.SemaphoreType.REGULAR,
        ],
        compiler_params=pltpu.CompilerParams(
            collective_id=0, has_side_effects=True, vmem_limit_bytes=56 * 1024 * 1024
        ),
    )(tas, tpb.T, plen, q, k, v, w, dn, up)


def solution(mesh):
    return jax.shard_map(
        on_device,
        mesh=mesh,
        in_specs=(
            P(("grp", "sp"), "tp"),
            P(("grp", "sp"), "tp"),
            P(("grp", "sp"), "tp"),
            P("grp", None),
            P("tp", "sp"),
            P("grp", None, ("tp", "sp")),
            P("grp", None, ("sp", "tp")),
            P(),
            P(),
        ),
        out_specs=P(("grp", "tp"), "sp"),
        check_vma=False,
    )
```

```python
import functools

import jax
import jax.numpy as jnp
from jax import lax
from jax.experimental import pallas as pl
from jax.experimental.pallas import tpu as pltpu
from jax.sharding import PartitionSpec as P

HS = 128
RANK = 64
BLOCK = 128
BLOCKS = 5
NSP = 4
NTP = 8
NCHIP = 4
NZ = 8
SLOTS = 4
HEADS = 8
ROWS = 160
HALF = 80
FEAT = 1024
COLS = 2048
SLICE = 256
PARTS = 4
PCOLS = COLS // PARTS
TILE = 256
STACK = 8
PIECES = ((0, 32), (32, 48))

adapter_scale = 0.5
big_negative = -1e30
MESH = pl.DeviceIdType.MESH
F32 = jnp.float32
BF16 = jnp.bfloat16


def copy_to(src, dst, ssem, rsem, **axis):
    return pltpu.make_async_remote_copy(
        src_ref=src, dst_ref=dst, send_sem=ssem, recv_sem=rsem, device_id=axis, device_id_type=MESH
    )


def kernel(
    tas, tpb, plen, q_hbm, k_hbm, v_hbm, w_hbm, dn_hbm, up_hbm, out_ref,
    qv, kv, vv, wv, dnv, upv, probs, att, keep, sibs, sibr, xs, xr, hop, fin,
    zs, zr0, zr1, cross, crossr, down, up2own, up2, lxs, lxr, lrs, lyx, lrr,
    lsem, kvs, kvr, atts, attr, zss, zrs, crs, crr, ups, upr,
    sbs, sbr, xss, xrs, txs, txr, lxss, lxrs, lys, lyr, z_in,
):
    sp = lax.axis_index("sp")
    tp = lax.axis_index("tp")
    grp = lax.axis_index("grp")
    chip = tp // 2
    core = tp % 2
    sib = tp + 1 - 2 * core
    y_lo = grp // NZ
    z = grp % NZ
    other = (1 - y_lo) * NZ + z
    zr = (zr0, zr1)
    right = (sp + 1) % NSP
    left = (sp + NSP - 1) % NSP

    loads = [
        pltpu.make_async_copy(k_hbm, kv.at[2], lsem.at[0]),
        pltpu.make_async_copy(q_hbm, qv, lsem.at[1]),
        pltpu.make_async_copy(v_hbm, vv.at[2], lsem.at[2]),
        pltpu.make_async_copy(dn_hbm, dnv, lsem.at[3]),
        pltpu.make_async_copy(up_hbm, upv, lsem.at[4]),
        pltpu.make_async_copy(w_hbm, wv, lsem.at[5]),
    ]
    barrier = pltpu.get_barrier_semaphore()
    for i in range(1, NSP):
        pl.semaphore_signal(barrier, inc=1, device_id={"sp": (sp + i) % NSP}, device_id_type=MESH)
    for i in range(1, NTP):
        pl.semaphore_signal(barrier, inc=1, device_id={"tp": (tp + i) % NTP}, device_id_type=MESH)
    pl.semaphore_signal(barrier, inc=1, device_id={"grp": other}, device_id_type=MESH)
    for i in range(1, NZ):
        @pl.when(z + i < NZ)
        def _():
            pl.semaphore_signal(barrier, inc=1, device_id={"grp": grp + i}, device_id_type=MESH)

    for c in loads:
        c.start()
    pl.semaphore_wait(barrier, (NSP - 1) + (NTP - 1) + 1 + z)
    for i in range(1, NZ):
        @pl.when(z >= i)
        def _():
            pl.semaphore_signal(z_in, inc=1, device_id={"grp": grp - i}, device_id_type=MESH)


    def kv_copy(m, i):
        return copy_to(
            (k_hbm, v_hbm)[m], (kv, vv)[m].at[2 - i], kvs.at[m, i - 1], kvr.at[m, i - 1],
            sp=(sp + i) % NSP,
        )

    for m in range(2):
        for i in (1, 2):
            @pl.when(sp + i < NSP)
            def _():
                kv_copy(m, i).start()

    loads[3].wait()
    loads[4].wait()

    def slot_of(g, b):
        return tas[tpb[b, g]]

    def pack(g, carry):
        pick = jnp.int32(0)
        for b in range(BLOCKS):
            slot = slot_of(g, b)
            pick = pick + jnp.where(slot // SLOTS == grp, slot % SLOTS, 0)
        zs[0, g % NZ, g // NZ] = dnv[pick]
        zs[1, g % NZ, g // NZ] = upv[pick]
        return carry

    lax.fori_loop(0, 2 * NZ, pack, 0)

    def z_copy(m, i):
        to = (z + i) % NZ
        return copy_to(
            zs.at[m, to], zr[m].at[z], zss.at[m, i - 1], zrs.at[m, i - 1], grp=y_lo * NZ + to
        )

    for m in range(2):
        for i in range(1, NZ):
            @pl.when(z + i >= NZ)
            def _():
                z_copy(m, i).start()

    for m in range(2):
        for j in range(2):
            zr[m][z, j] = zs[m, z, j]

    def kv_ready(m):
        for i in (1, 2):
            @pl.when(sp >= i)
            def _():
                kv_copy(m, i).wait_recv()

            @pl.when(sp < i)
            def _():
                (kv, vv)[m][2 - i] = jnp.zeros((ROWS, HS), BF16)

    loads[0].wait()
    loads[1].wait()
    kv_ready(0)
    end0 = plen[0, 0]
    end1 = end0 + plen[0, 1]
    keys = kv[...].reshape(3 * ROWS, HS)
    for h in range(2):
        qpos = sp * ROWS + h * HALF + lax.broadcasted_iota(jnp.int32, (HALF, 3 * ROWS), 0)
        kpos = (sp - 2) * ROWS + lax.broadcasted_iota(jnp.int32, (HALF, 3 * ROWS), 1)
        first = jnp.where(qpos >= end1, end1, jnp.where(qpos >= end0, end0, 0))
        allowed = (kpos <= qpos) & (kpos >= first)
        for n in range(0, HEADS, STACK):
            qh = jnp.concatenate(
                [qv[h * HALF:(h + 1) * HALF, m * HS:(m + 1) * HS] for m in range(n, n + STACK)], axis=0
            )
            s = lax.dot_general(qh, keys, (((1,), (1,)), ((), ())), preferred_element_type=F32)
            s = jnp.where(
                allowed[None], s.reshape(STACK, HALF, 3 * ROWS) * HS ** -0.5, big_negative
            )
            p = jnp.exp(s - jnp.max(s, axis=2, keepdims=True))
            probs[h, n * HALF:(n + STACK) * HALF] = p.astype(BF16).reshape(STACK * HALF, 3 * ROWS)
    loads[2].wait()
    kv_ready(1)
    vals = jnp.concatenate(
        [vv[...].reshape(3 * ROWS, HS), jnp.ones((3 * ROWS, HS), BF16)], axis=1
    )

    def first_copy(side):
        return copy_to(
            att.at[0, side], att.at[1, side], atts.at[side, 0], attr.at[side, 0],
            sp=(right, left)[side],
        )

    def later_copy(side, piece):
        rows = pl.ds(*PIECES[piece])
        return copy_to(
            att.at[0, 1 - side, rows], att.at[3, 1 - side, rows],
            atts.at[side, 1 + piece], attr.at[side, 1 + piece],
            sp=(right, left)[side],
        )

    def relay(side):
        return copy_to(
            att.at[1, side], att.at[2, side], atts.at[side, 3], attr.at[side, 3],
            sp=(right, left)[side],
        )

    for h in range(2):
        for n in range(0, HEADS, STACK):
            o = jnp.dot(
                probs[h, n * HALF:(n + STACK) * HALF], vals, preferred_element_type=F32
            )
            o = (o[:, :HS] / o[:, HS:]).astype(BF16)
            for m in range(STACK):
                att[0, h, :, (n + m) * HS:(n + m + 1) * HS] = o[m * HALF:(m + 1) * HALF]
        first_copy(h).start()
    for side in range(2):
        later_copy(side, 0).start()

    @pl.when(z < NZ - 1)
    def _():
        pl.semaphore_wait(z_in, NZ - 1 - z)

    for m in range(2):
        for i in range(1, NZ):
            @pl.when(z + i < NZ)
            def _():
                z_copy(m, i).start()

    loads[5].wait()

    shift = 2 * core - 1
    keep_block = [sp, (sp + NSP + shift) % NSP, (sp + 2) % NSP, (sp + NSP - shift) % NSP]

    def sib_copy(k, part):
        cols = pl.ds(part * PCOLS, PCOLS)
        return copy_to(sibs.at[k, :, cols], sibr.at[k, :, cols], sbs.at[k, part], sbr.at[k, part], tp=sib)

    def product_part(k, part):
        for n in range(PCOLS // TILE):
            cols = pl.ds(part * PCOLS + n * TILE, TILE)
            v = jnp.dot(
                att[k].reshape(ROWS, FEAT), wv[:, cols], preferred_element_type=F32
            )
            keep[k, :, cols] = jnp.where(core == 0, v[:HALF], v[HALF:])
            sibs[k, :, cols] = jnp.where(core == 0, v[HALF:], v[:HALF]).astype(BF16)
        sib_copy(k, part).start()

    def product(k):
        for part in range(PARTS):
            product_part(k, part)

    def x_copy(k, part):
        cols = pl.ds(part * PCOLS, PCOLS)
        rel = (chip + NCHIP - keep_block[k] + NCHIP - 1) % NCHIP
        return copy_to(
            xs.at[k, :, cols], xr.at[rel, :, cols], xss.at[k, part], xrs.at[rel, part],
            tp=2 * keep_block[k] + core,
        )

    def x_part(k, part):
        cols = pl.ds(part * PCOLS, PCOLS)
        sib_copy(k, part).wait_recv()
        total = keep[k, :, cols] + sibr[k, :, cols].astype(F32)

        @pl.when(keep_block[k] == chip)
        def _():
            fin[:, cols] = total

        @pl.when(keep_block[k] != chip)
        def _():
            xs[k, :, cols] = total.astype(BF16)
            x_copy(k, part).start()

    def x_phase(k):
        for part in range(PARTS):
            x_part(k, part)

    far = (sp + 2) % NSP
    place = (chip + NCHIP - far) % NCHIP

    def tree_copy(part):
        cols = pl.ds(part * PCOLS, PCOLS)
        side = part // (PARTS // 2)
        to = (far + (1, NCHIP - 1)[side]) % NCHIP
        return copy_to(
            xs.at[2, :, cols], hop.at[part % (PARTS // 2)], txs.at[part], txr.at[part % (PARTS // 2)],
            tp=2 * to + core,
        )

    def far_phase():
        k = 2
        for part in range(PARTS):
            cols = pl.ds(part * PCOLS, PCOLS)
            side = part // (PARTS // 2)
            sib_copy(k, part).wait_recv()
            total = keep[k, :, cols] + sibr[k, :, cols].astype(F32)

            @pl.when(place == 0)
            def _():
                fin[:, cols] = total

            @pl.when(place == 2)
            def _():
                xs[k, :, cols] = total.astype(BF16)
                tree_copy(part).start()

            @pl.when(place == (3, 1)[side])
            def _():
                xs[k, :, cols] = total.astype(BF16)
                x_copy(k, part).start()

            @pl.when(place == (1, 3)[side])
            def _():
                keep[k, :, cols] = total

        for part in range(PARTS):
            cols = pl.ds(part * PCOLS, PCOLS)
            side = part // (PARTS // 2)

            @pl.when(place == (1, 3)[side])
            def _():
                tree_copy(part).wait_recv()
                total = keep[k, :, cols] + hop[part % (PARTS // 2)].astype(F32)
                xs[k, :, cols] = total.astype(BF16)
                x_copy(k, part).start()

        @pl.when(place == 0)
        def _():
            xr[1] = jnp.zeros((HALF, COLS), BF16)

    lane = lax.broadcasted_iota(jnp.int32, (HALF, 2 * RANK), 1)
    row = lax.broadcasted_iota(jnp.int32, (HALF, 2 * RANK), 0)
    features = pl.ds(pl.multiple_of(sp * SLICE, SLICE), SLICE)
    blocks_of = [(sp, sp), (left, right), (far, far), (right, left)]

    def low_copy(k, h):
        to = 2 * blocks_of[k][h] + h
        rel = (tp + NTP - to + NTP - 1) % NTP
        return copy_to(lxs.at[k, h], lxr.at[rel], lxss.at[k, h], lxrs.at[rel], tp=to)

    def low_rank(k):
        for h in range(2):
            sb = blocks_of[k][h]
            pair = down[pl.ds(sb, 2)].reshape(2 * RANK, SLICE)
            lr = lax.dot_general(
                att[k, h, :, features], pair, (((1,), (1,)), ((), ())), preferred_element_type=F32
            )
            early = (row + h * HALF < BLOCK - (ROWS - BLOCK) * sb).astype(jnp.int32)
            firsts = (lane < RANK).astype(jnp.int32)
            lr = jnp.where(early == firsts, lr, 0.0)

            @pl.when(2 * sb + h == tp)
            def _():
                lrs[...] = lr

            @pl.when(2 * sb + h != tp)
            def _():
                lxs[k, h] = lr.astype(BF16)
                low_copy(k, h).start()

    def cross_copy(m):
        return copy_to(cross.at[m], crossr.at[m], crs.at[m], crr.at[m], grp=other)

    def cross_send(m):
        for i in range(1, NZ):
            z_copy(m, i).wait_recv()

        def fill(b, carry):
            owner = slot_of(other, b) // SLOTS
            cross[m, b] = zr[m][owner % NZ, 1 - y_lo]
            return carry

        lax.fori_loop(0, BLOCKS, fill, 0)
        cross_copy(m).start()

    def cross_take(m, dst):
        cross_copy(m).wait_recv()

        def fill(b, carry):
            owner = slot_of(grp, b) // SLOTS
            dst[b] = jnp.where(owner // NZ == y_lo, zr[m][owner % NZ, y_lo], crossr[m, b])
            return carry

        lax.fori_loop(0, BLOCKS, fill, 0)

    def up_copy(i):
        to = (chip + i) % NCHIP
        return copy_to(
            up2own.at[pl.ds(to, 2)], up2.at[tp], ups.at[i - 1], upr.at[i - 1], tp=2 * to + core
        )

    def up_share(i):
        at = 2 * ((chip + NCHIP - i) % NCHIP) + core
        return copy_to(
            up2.at[at], up2.at[at], ups.at[NCHIP - 1 + i], upr.at[NCHIP - 1 + i], tp=sib
        )

    product(0)

    for side in range(2):
        first_copy(side).wait_recv()
        relay(side).start()
    for side in range(2):
        later_copy(side, 1).start()
    x_phase(0)
    product(1)
    x_phase(1)
    cross_send(0)

    for side in range(2):
        relay(side).wait_recv()
    product(2)
    far_phase()
    cross_take(0, down)
    for k in range(3):
        low_rank(k)
    cross_send(1)

    for side in range(2):
        for piece in range(2):
            later_copy(side, piece).wait_recv()
    low_rank(3)
    for part in range(PARTS):
        product_part(3, part)
        if part > 0:
            x_part(3, part - 1)
    x_part(3, PARTS - 1)

    for rel in range(NTP - 1):
        copy_to(lxs.at[0, 0], lxr.at[rel], lxss.at[0, 0], lxrs.at[rel], tp=sib).wait_recv()
    low = lrs[...]
    for rel in range(NTP - 1):
        low = low + lxr[rel].astype(F32)
    lrs[...] = low
    lyx[...] = low.astype(BF16)

    def ly_copy(i):
        return copy_to(lyx, lrr.at[i - 1], lys.at[i - 1], lyr.at[i - 1], sp=(sp + i) % NSP)

    for i in range(1, NSP):
        ly_copy(i).start()

    cross_take(1, up2own)
    for i in range(1, NCHIP):
        up_copy(i).start()
    up2[tp] = up2own[pl.ds(chip, 2)]
    up_share(0).start()
    for i in range(1, NCHIP):
        up_copy(i).wait_recv()
        up_share(i).start()
    for i in range(1, NSP):
        ly_copy(i).wait_recv()
    low = lrs[...]
    for i in range(NSP - 1):
        low = low + lrr[i].astype(F32)
    low = low.astype(BF16)
    for i in range(NCHIP):
        up_share(i).wait_recv()
    for part in range(PARTS):
        cols = pl.ds(part * PCOLS, PCOLS)
        for rel in range(NCHIP - 1):
            came = copy_to(
                xs.at[0, :, cols], xr.at[rel, :, cols], xss.at[0, part], xrs.at[rel, part], tp=sib
            )
            if rel == 1:
                @pl.when(place != 0)
                def _():
                    came.wait_recv()
            else:
                came.wait_recv()
        for n in range(PCOLS // SLICE):
            j = part * (PCOLS // SLICE) + n
            c = pl.ds(j * SLICE, SLICE)
            delta = jnp.dot(low, up2[j].reshape(2 * RANK, SLICE), preferred_element_type=F32)
            base = fin[:, c] + (
                xr[0, :, c].astype(F32) + xr[1, :, c].astype(F32) + xr[2, :, c].astype(F32)
            )
            out_ref[:, c] = (base + adapter_scale * delta).astype(BF16)

    for m in range(2):
        for i in (1, 2):
            @pl.when(sp + i < NSP)
            def _():
                kv_copy(m, i).wait_send()
        for i in range(1, NZ):
            z_copy(m, i).wait_send()
        cross_copy(m).wait_send()
    for side in range(2):
        first_copy(side).wait_send()
        relay(side).wait_send()
        for piece in range(2):
            later_copy(side, piece).wait_send()
    for i in range(1, NCHIP):
        up_copy(i).wait_send()
    for i in range(NCHIP):
        up_share(i).wait_send()
    for k in range(4):
        for part in range(PARTS):
            sib_copy(k, part).wait_send()

        if k == 2:
            @pl.when(place == 2)
            def _():
                for part in range(PARTS):
                    tree_copy(part).wait_send()

            @pl.when(place % 2 == 1)
            def _():
                for part in range(PARTS):
                    x_copy(k, part).wait_send()
        else:
            @pl.when(keep_block[k] != chip)
            def _():
                for part in range(PARTS):
                    x_copy(k, part).wait_send()

        for h in range(2):
            @pl.when(2 * blocks_of[k][h] + h != tp)
            def _():
                low_copy(k, h).wait_send()
    for i in range(1, NSP):
        ly_copy(i).wait_send()


def on_device(q, k, v, plen, w, dn, up, tas, tpb):
    smem = pl.BlockSpec(memory_space=pltpu.SMEM)
    anym = pl.BlockSpec(memory_space=pl.ANY)
    V = pltpu.VMEM
    D = pltpu.SemaphoreType.DMA
    return pl.pallas_call(
        kernel,
        out_shape=jax.ShapeDtypeStruct((HALF, COLS), BF16),
        in_specs=[smem] * 3 + [anym] * 6,
        out_specs=pl.BlockSpec(memory_space=pltpu.VMEM),
        scratch_shapes=[
            V((ROWS, FEAT), BF16),
            V((3, ROWS, HS), BF16),
            V((3, ROWS, HS), BF16),
            V((FEAT, COLS), BF16),
            V((SLOTS, RANK, SLICE), BF16),
            V((SLOTS, RANK, SLICE), BF16),
            V((2, HEADS * HALF, 3 * ROWS), BF16),
            V((4, 2, HALF, FEAT), BF16),
            V((4, HALF, COLS), F32),
            V((4, HALF, COLS), BF16),
            V((4, HALF, COLS), BF16),
            V((4, HALF, COLS), BF16),
            V((NCHIP - 1, HALF, COLS), BF16),
            V((PARTS // 2, HALF, PCOLS), BF16),
            V((HALF, COLS), F32),
            V((2, NZ, 2, RANK, SLICE), BF16),
            V((NZ, 2, RANK, SLICE), BF16),
            V((NZ, 2, RANK, SLICE), BF16),
            V((2, BLOCKS, RANK, SLICE), BF16),
            V((2, BLOCKS, RANK, SLICE), BF16),
            V((BLOCKS, RANK, SLICE), BF16),
            V((BLOCKS, RANK, SLICE), BF16),
            V((NTP, 2, RANK, SLICE), BF16),
            V((4, 2, HALF, 2 * RANK), BF16),
            V((NTP - 1, HALF, 2 * RANK), BF16),
            V((HALF, 2 * RANK), F32),
            V((HALF, 2 * RANK), BF16),
            V((NSP - 1, HALF, 2 * RANK), BF16),
            D((6,)),
            D((2, 2)), D((2, 2)),
            D((2, 4)), D((2, 4)),
            D((2, NZ - 1)), D((2, NZ - 1)),
            D((2,)), D((2,)),
            D((2 * NCHIP - 1,)), D((2 * NCHIP - 1,)),
            D((4, PARTS)), D((4, PARTS)),
            D((4, PARTS)), D((NCHIP - 1, PARTS)),
            D((PARTS,)), D((PARTS // 2,)),
            D((4, 2)), D((NTP - 1,)),
            D((NSP - 1,)), D((NSP - 1,)),
            pltpu.SemaphoreType.REGULAR,
        ],
        compiler_params=pltpu.CompilerParams(
            collective_id=0, has_side_effects=True, vmem_limit_bytes=56 * 1024 * 1024
        ),
    )(tas, tpb.T, plen, q, k, v, w, dn, up)


def solution(mesh):
    return jax.shard_map(
        on_device,
        mesh=mesh,
        in_specs=(
            P(("grp", "sp"), "tp"),
            P(("grp", "sp"), "tp"),
            P(("grp", "sp"), "tp"),
            P("grp", None),
            P("tp", "sp"),
            P("grp", None, ("tp", "sp")),
            P("grp", None, ("sp", "tp")),
            P(),
            P(),
        ),
        out_specs=P(("grp", "tp"), "sp"),
        check_vma=False,
    )
```

```python
import functools

import jax
import jax.numpy as jnp
from jax import lax
from jax.experimental import pallas as pl
from jax.experimental.pallas import tpu as pltpu
from jax.sharding import PartitionSpec as P

HS = 128
RANK = 64
BLOCK = 128
BLOCKS = 5
NSP = 4
NTP = 8
NCHIP = 4
NZ = 8
SLOTS = 4
HEADS = 8
ROWS = 160
HALF = 80
FEAT = 1024
COLS = 2048
SLICE = 256
PARTS = 4
PCOLS = COLS // PARTS
TILE = 256
STACK = 8
PIECES = ((0, 32), (32, 48))

adapter_scale = 0.5
big_negative = -1e30
MESH = pl.DeviceIdType.MESH
F32 = jnp.float32
BF16 = jnp.bfloat16


def copy_to(src, dst, ssem, rsem, **axis):
    return pltpu.make_async_remote_copy(
        src_ref=src, dst_ref=dst, send_sem=ssem, recv_sem=rsem, device_id=axis, device_id_type=MESH
    )


def kernel(
    tas, tpb, plen, q_hbm, k_hbm, v_hbm, w_hbm, dn_hbm, up_hbm, out_ref,
    qv, kv, vv, wv, dnv, upv, probs, att, keep, sibs, sibr, xs, xr, hop, fin,
    zs, zr0, zr1, cross, crossr, down, up2own, up2, lxs, lxr, lrs, lyx, lrr,
    lsem, kvs, kvr, atts, attr, zss, zrs, crs, crr, ups, upr,
    sbs, sbr, xss, xrs, txs, txr, lxss, lxrs, lys, lyr, z_in,
):
    sp = lax.axis_index("sp")
    tp = lax.axis_index("tp")
    grp = lax.axis_index("grp")
    chip = tp // 2
    core = tp % 2
    sib = tp + 1 - 2 * core
    y_lo = grp // NZ
    z = grp % NZ
    other = (1 - y_lo) * NZ + z
    zr = (zr0, zr1)
    right = (sp + 1) % NSP
    left = (sp + NSP - 1) % NSP

    loads = [
        pltpu.make_async_copy(k_hbm, kv.at[2], lsem.at[0]),
        pltpu.make_async_copy(q_hbm, qv, lsem.at[1]),
        pltpu.make_async_copy(v_hbm, vv.at[2], lsem.at[2]),
        pltpu.make_async_copy(dn_hbm, dnv, lsem.at[3]),
        pltpu.make_async_copy(up_hbm, upv, lsem.at[4]),
        pltpu.make_async_copy(w_hbm, wv, lsem.at[5]),
    ]
    barrier = pltpu.get_barrier_semaphore()
    for i in range(1, NSP):
        pl.semaphore_signal(barrier, inc=1, device_id={"sp": (sp + i) % NSP}, device_id_type=MESH)
    for i in range(1, NTP):
        pl.semaphore_signal(barrier, inc=1, device_id={"tp": (tp + i) % NTP}, device_id_type=MESH)
    pl.semaphore_signal(barrier, inc=1, device_id={"grp": other}, device_id_type=MESH)
    for i in range(1, NZ):
        @pl.when(z + i < NZ)
        def _():
            pl.semaphore_signal(barrier, inc=1, device_id={"grp": grp + i}, device_id_type=MESH)

    for c in loads:
        c.start()
    pl.semaphore_wait(barrier, (NSP - 1) + (NTP - 1) + 1 + z)
    for i in range(1, NZ):
        @pl.when(z >= i)
        def _():
            pl.semaphore_signal(z_in, inc=1, device_id={"grp": grp - i}, device_id_type=MESH)


    def kv_copy(m, i):
        return copy_to(
            (k_hbm, v_hbm)[m], (kv, vv)[m].at[2 - i], kvs.at[m, i - 1], kvr.at[m, i - 1],
            sp=(sp + i) % NSP,
        )

    for m in range(2):
        for i in (1, 2):
            @pl.when(sp + i < NSP)
            def _():
                kv_copy(m, i).start()

    loads[3].wait()
    loads[4].wait()

    def slot_of(g, b):
        return tas[tpb[b, g]]

    def pack(g, carry):
        pick = jnp.int32(0)
        for b in range(BLOCKS):
            slot = slot_of(g, b)
            pick = pick + jnp.where(slot // SLOTS == grp, slot % SLOTS, 0)
        zs[0, g % NZ, g // NZ] = dnv[pick]
        zs[1, g % NZ, g // NZ] = upv[pick]
        return carry

    lax.fori_loop(0, 2 * NZ, pack, 0)

    def z_copy(m, i):
        to = (z + i) % NZ
        return copy_to(
            zs.at[m, to], zr[m].at[z], zss.at[m, i - 1], zrs.at[m, i - 1], grp=y_lo * NZ + to
        )

    for m in (1, 0):
        for i in range(1, NZ):
            @pl.when(z + i >= NZ)
            def _():
                z_copy(m, i).start()

    for m in range(2):
        for j in range(2):
            zr[m][z, j] = zs[m, z, j]

    def kv_ready(m):
        for i in (1, 2):
            @pl.when(sp >= i)
            def _():
                kv_copy(m, i).wait_recv()

            @pl.when(sp < i)
            def _():
                (kv, vv)[m][2 - i] = jnp.zeros((ROWS, HS), BF16)

    loads[0].wait()
    loads[1].wait()
    kv_ready(0)
    end0 = plen[0, 0]
    end1 = end0 + plen[0, 1]
    keys = kv[...].reshape(3 * ROWS, HS)
    for h in range(2):
        qpos = sp * ROWS + h * HALF + lax.broadcasted_iota(jnp.int32, (HALF, 3 * ROWS), 0)
        kpos = (sp - 2) * ROWS + lax.broadcasted_iota(jnp.int32, (HALF, 3 * ROWS), 1)
        first = jnp.where(qpos >= end1, end1, jnp.where(qpos >= end0, end0, 0))
        allowed = (kpos <= qpos) & (kpos >= first)
        for n in range(0, HEADS, STACK):
            qh = jnp.concatenate(
                [qv[h * HALF:(h + 1) * HALF, m * HS:(m + 1) * HS] for m in range(n, n + STACK)], axis=0
            )
            s = lax.dot_general(qh, keys, (((1,), (1,)), ((), ())), preferred_element_type=F32)
            s = jnp.where(
                allowed[None], s.reshape(STACK, HALF, 3 * ROWS) * HS ** -0.5, big_negative
            )
            p = jnp.exp(s - jnp.max(s, axis=2, keepdims=True))
            probs[h, n * HALF:(n + STACK) * HALF] = p.astype(BF16).reshape(STACK * HALF, 3 * ROWS)
    loads[2].wait()
    kv_ready(1)
    vals = jnp.concatenate(
        [vv[...].reshape(3 * ROWS, HS), jnp.ones((3 * ROWS, HS), BF16)], axis=1
    )

    def first_copy(side):
        return copy_to(
            att.at[0, side], att.at[1, side], atts.at[side, 0], attr.at[side, 0],
            sp=(right, left)[side],
        )

    def later_copy(side, piece):
        rows = pl.ds(*PIECES[piece])
        return copy_to(
            att.at[0, 1 - side, rows], att.at[3, 1 - side, rows],
            atts.at[side, 1 + piece], attr.at[side, 1 + piece],
            sp=(right, left)[side],
        )

    def relay(side):
        return copy_to(
            att.at[1, side], att.at[2, side], atts.at[side, 3], attr.at[side, 3],
            sp=(right, left)[side],
        )

    for h in range(2):
        for n in range(0, HEADS, STACK):
            o = jnp.dot(
                probs[h, n * HALF:(n + STACK) * HALF], vals, preferred_element_type=F32
            )
            o = (o[:, :HS] / o[:, HS:]).astype(BF16)
            for m in range(STACK):
                att[0, h, :, (n + m) * HS:(n + m + 1) * HS] = o[m * HALF:(m + 1) * HALF]
        first_copy(h).start()
    for side in range(2):
        later_copy(side, 0).start()

    @pl.when(z < NZ - 1)
    def _():
        pl.semaphore_wait(z_in, NZ - 1 - z)

    for m in (1, 0):
        for i in range(1, NZ):
            @pl.when(z + i < NZ)
            def _():
                z_copy(m, i).start()

    loads[5].wait()

    shift = 2 * core - 1
    keep_block = [sp, (sp + NSP + shift) % NSP, (sp + 2) % NSP, (sp + NSP - shift) % NSP]

    def sib_copy(k, part):
        cols = pl.ds(part * PCOLS, PCOLS)
        return copy_to(sibs.at[k, :, cols], sibr.at[k, :, cols], sbs.at[k, part], sbr.at[k, part], tp=sib)

    def product_part(k, part):
        for n in range(PCOLS // TILE):
            cols = pl.ds(part * PCOLS + n * TILE, TILE)
            v = jnp.dot(
                att[k].reshape(ROWS, FEAT), wv[:, cols], preferred_element_type=F32
            )
            keep[k, :, cols] = jnp.where(core == 0, v[:HALF], v[HALF:])
            sibs[k, :, cols] = jnp.where(core == 0, v[HALF:], v[:HALF]).astype(BF16)
        sib_copy(k, part).start()

    def product(k):
        for part in range(PARTS):
            product_part(k, part)

    def x_copy(k, part):
        cols = pl.ds(part * PCOLS, PCOLS)
        rel = (chip + NCHIP - keep_block[k] + NCHIP - 1) % NCHIP
        return copy_to(
            xs.at[k, :, cols], xr.at[rel, :, cols], xss.at[k, part], xrs.at[rel, part],
            tp=2 * keep_block[k] + core,
        )

    def x_part(k, part):
        cols = pl.ds(part * PCOLS, PCOLS)
        sib_copy(k, part).wait_recv()
        total = keep[k, :, cols] + sibr[k, :, cols].astype(F32)

        @pl.when(keep_block[k] == chip)
        def _():
            fin[:, cols] = total

        @pl.when(keep_block[k] != chip)
        def _():
            xs[k, :, cols] = total.astype(BF16)
            x_copy(k, part).start()

    def x_phase(k):
        for part in range(PARTS):
            x_part(k, part)

    far = (sp + 2) % NSP
    place = (chip + NCHIP - far) % NCHIP

    def tree_copy(part):
        cols = pl.ds(part * PCOLS, PCOLS)
        side = part // (PARTS // 2)
        to = (far + (1, NCHIP - 1)[side]) % NCHIP
        return copy_to(
            xs.at[2, :, cols], hop.at[part % (PARTS // 2)], txs.at[part], txr.at[part % (PARTS // 2)],
            tp=2 * to + core,
        )

    def far_phase():
        k = 2
        for part in range(PARTS):
            cols = pl.ds(part * PCOLS, PCOLS)
            side = part // (PARTS // 2)
            sib_copy(k, part).wait_recv()
            total = keep[k, :, cols] + sibr[k, :, cols].astype(F32)

            @pl.when(place == 0)
            def _():
                fin[:, cols] = total

            @pl.when(place == 2)
            def _():
                xs[k, :, cols] = total.astype(BF16)
                tree_copy(part).start()

            @pl.when(place == (3, 1)[side])
            def _():
                xs[k, :, cols] = total.astype(BF16)
                x_copy(k, part).start()

            @pl.when(place == (1, 3)[side])
            def _():
                keep[k, :, cols] = total

        for part in range(PARTS):
            cols = pl.ds(part * PCOLS, PCOLS)
            side = part // (PARTS // 2)

            @pl.when(place == (1, 3)[side])
            def _():
                tree_copy(part).wait_recv()
                total = keep[k, :, cols] + hop[part % (PARTS // 2)].astype(F32)
                xs[k, :, cols] = total.astype(BF16)
                x_copy(k, part).start()

        @pl.when(place == 0)
        def _():
            xr[1] = jnp.zeros((HALF, COLS), BF16)

    lane = lax.broadcasted_iota(jnp.int32, (HALF, 2 * RANK), 1)
    row = lax.broadcasted_iota(jnp.int32, (HALF, 2 * RANK), 0)
    features = pl.ds(pl.multiple_of(sp * SLICE, SLICE), SLICE)
    blocks_of = [(sp, sp), (left, right), (far, far), (right, left)]

    def low_copy(k, h):
        to = 2 * blocks_of[k][h] + h
        rel = (tp + NTP - to + NTP - 1) % NTP
        return copy_to(lxs.at[k, h], lxr.at[rel], lxss.at[k, h], lxrs.at[rel], tp=to)

    def low_rank(k):
        for h in range(2):
            sb = blocks_of[k][h]
            pair = down[pl.ds(sb, 2)].reshape(2 * RANK, SLICE)
            lr = lax.dot_general(
                att[k, h, :, features], pair, (((1,), (1,)), ((), ())), preferred_element_type=F32
            )
            early = (row + h * HALF < BLOCK - (ROWS - BLOCK) * sb).astype(jnp.int32)
            firsts = (lane < RANK).astype(jnp.int32)
            lr = jnp.where(early == firsts, lr, 0.0)

            @pl.when(2 * sb + h == tp)
            def _():
                lrs[...] = lr

            @pl.when(2 * sb + h != tp)
            def _():
                lxs[k, h] = lr.astype(BF16)
                low_copy(k, h).start()

    def cross_copy(m):
        return copy_to(cross.at[m], crossr.at[m], crs.at[m], crr.at[m], grp=other)

    def cross_send(m):
        for i in range(1, NZ):
            z_copy(m, i).wait_recv()

        def fill(b, carry):
            owner = slot_of(other, b) // SLOTS
            cross[m, b] = zr[m][owner % NZ, 1 - y_lo]
            return carry

        lax.fori_loop(0, BLOCKS, fill, 0)
        cross_copy(m).start()

    def cross_take(m, dst):
        cross_copy(m).wait_recv()

        def fill(b, carry):
            owner = slot_of(grp, b) // SLOTS
            dst[b] = jnp.where(owner // NZ == y_lo, zr[m][owner % NZ, y_lo], crossr[m, b])
            return carry

        lax.fori_loop(0, BLOCKS, fill, 0)

    def up_copy(i):
        to = (chip + i) % NCHIP
        return copy_to(
            up2own.at[pl.ds(to, 2)], up2.at[tp], ups.at[i - 1], upr.at[i - 1], tp=2 * to + core
        )

    def up_share(i):
        at = 2 * ((chip + NCHIP - i) % NCHIP) + core
        return copy_to(
            up2.at[at], up2.at[at], ups.at[NCHIP - 1 + i], upr.at[NCHIP - 1 + i], tp=sib
        )

    product(0)

    for side in range(2):
        first_copy(side).wait_recv()
        relay(side).start()
    for side in range(2):
        later_copy(side, 1).start()
    x_phase(0)
    product(1)
    x_phase(1)
    cross_send(0)

    for side in range(2):
        relay(side).wait_recv()
    product(2)
    far_phase()
    cross_take(0, down)
    for k in range(3):
        low_rank(k)
    cross_send(1)

    for side in range(2):
        for piece in range(2):
            later_copy(side, piece).wait_recv()
    low_rank(3)
    for part in range(PARTS):
        product_part(3, part)
        if part > 0:
            x_part(3, part - 1)
    x_part(3, PARTS - 1)

    for rel in range(NTP - 1):
        copy_to(lxs.at[0, 0], lxr.at[rel], lxss.at[0, 0], lxrs.at[rel], tp=sib).wait_recv()
    low = lrs[...]
    for rel in range(NTP - 1):
        low = low + lxr[rel].astype(F32)
    lrs[...] = low
    lyx[...] = low.astype(BF16)

    def ly_copy(i):
        return copy_to(lyx, lrr.at[i - 1], lys.at[i - 1], lyr.at[i - 1], sp=(sp + i) % NSP)

    for i in range(1, NSP):
        ly_copy(i).start()

    cross_take(1, up2own)
    for i in range(1, NCHIP):
        up_copy(i).start()
    up2[tp] = up2own[pl.ds(chip, 2)]
    up_share(0).start()
    for i in range(1, NCHIP):
        up_copy(i).wait_recv()
        up_share(i).start()
    for i in range(1, NSP):
        ly_copy(i).wait_recv()
    low = lrs[...]
    for i in range(NSP - 1):
        low = low + lrr[i].astype(F32)
    low = low.astype(BF16)
    for i in range(NCHIP):
        up_share(i).wait_recv()
    for part in range(PARTS):
        cols = pl.ds(part * PCOLS, PCOLS)
        for rel in range(NCHIP - 1):
            came = copy_to(
                xs.at[0, :, cols], xr.at[rel, :, cols], xss.at[0, part], xrs.at[rel, part], tp=sib
            )
            if rel == 1:
                @pl.when(place != 0)
                def _():
                    came.wait_recv()
            else:
                came.wait_recv()
        for n in range(PCOLS // SLICE):
            j = part * (PCOLS // SLICE) + n
            c = pl.ds(j * SLICE, SLICE)
            delta = jnp.dot(low, up2[j].reshape(2 * RANK, SLICE), preferred_element_type=F32)
            base = fin[:, c] + (
                xr[0, :, c].astype(F32) + xr[1, :, c].astype(F32) + xr[2, :, c].astype(F32)
            )
            out_ref[:, c] = (base + adapter_scale * delta).astype(BF16)

    for m in range(2):
        for i in (1, 2):
            @pl.when(sp + i < NSP)
            def _():
                kv_copy(m, i).wait_send()
        for i in range(1, NZ):
            z_copy(m, i).wait_send()
        cross_copy(m).wait_send()
    for side in range(2):
        first_copy(side).wait_send()
        relay(side).wait_send()
        for piece in range(2):
            later_copy(side, piece).wait_send()
    for i in range(1, NCHIP):
        up_copy(i).wait_send()
    for i in range(NCHIP):
        up_share(i).wait_send()
    for k in range(4):
        for part in range(PARTS):
            sib_copy(k, part).wait_send()

        if k == 2:
            @pl.when(place == 2)
            def _():
                for part in range(PARTS):
                    tree_copy(part).wait_send()

            @pl.when(place % 2 == 1)
            def _():
                for part in range(PARTS):
                    x_copy(k, part).wait_send()
        else:
            @pl.when(keep_block[k] != chip)
            def _():
                for part in range(PARTS):
                    x_copy(k, part).wait_send()

        for h in range(2):
            @pl.when(2 * blocks_of[k][h] + h != tp)
            def _():
                low_copy(k, h).wait_send()
    for i in range(1, NSP):
        ly_copy(i).wait_send()


def on_device(q, k, v, plen, w, dn, up, tas, tpb):
    smem = pl.BlockSpec(memory_space=pltpu.SMEM)
    anym = pl.BlockSpec(memory_space=pl.ANY)
    V = pltpu.VMEM
    D = pltpu.SemaphoreType.DMA
    return pl.pallas_call(
        kernel,
        out_shape=jax.ShapeDtypeStruct((HALF, COLS), BF16),
        in_specs=[smem] * 3 + [anym] * 6,
        out_specs=pl.BlockSpec(memory_space=pltpu.VMEM),
        scratch_shapes=[
            V((ROWS, FEAT), BF16),
            V((3, ROWS, HS), BF16),
            V((3, ROWS, HS), BF16),
            V((FEAT, COLS), BF16),
            V((SLOTS, RANK, SLICE), BF16),
            V((SLOTS, RANK, SLICE), BF16),
            V((2, HEADS * HALF, 3 * ROWS), BF16),
            V((4, 2, HALF, FEAT), BF16),
            V((4, HALF, COLS), F32),
            V((4, HALF, COLS), BF16),
            V((4, HALF, COLS), BF16),
            V((4, HALF, COLS), BF16),
            V((NCHIP - 1, HALF, COLS), BF16),
            V((PARTS // 2, HALF, PCOLS), BF16),
            V((HALF, COLS), F32),
            V((2, NZ, 2, RANK, SLICE), BF16),
            V((NZ, 2, RANK, SLICE), BF16),
            V((NZ, 2, RANK, SLICE), BF16),
            V((2, BLOCKS, RANK, SLICE), BF16),
            V((2, BLOCKS, RANK, SLICE), BF16),
            V((BLOCKS, RANK, SLICE), BF16),
            V((BLOCKS, RANK, SLICE), BF16),
            V((NTP, 2, RANK, SLICE), BF16),
            V((4, 2, HALF, 2 * RANK), BF16),
            V((NTP - 1, HALF, 2 * RANK), BF16),
            V((HALF, 2 * RANK), F32),
            V((HALF, 2 * RANK), BF16),
            V((NSP - 1, HALF, 2 * RANK), BF16),
            D((6,)),
            D((2, 2)), D((2, 2)),
            D((2, 4)), D((2, 4)),
            D((2, NZ - 1)), D((2, NZ - 1)),
            D((2,)), D((2,)),
            D((2 * NCHIP - 1,)), D((2 * NCHIP - 1,)),
            D((4, PARTS)), D((4, PARTS)),
            D((4, PARTS)), D((NCHIP - 1, PARTS)),
            D((PARTS,)), D((PARTS // 2,)),
            D((4, 2)), D((NTP - 1,)),
            D((NSP - 1,)), D((NSP - 1,)),
            pltpu.SemaphoreType.REGULAR,
        ],
        compiler_params=pltpu.CompilerParams(
            collective_id=0, has_side_effects=True, vmem_limit_bytes=56 * 1024 * 1024
        ),
    )(tas, tpb.T, plen, q, k, v, w, dn, up)


def solution(mesh):
    return jax.shard_map(
        on_device,
        mesh=mesh,
        in_specs=(
            P(("grp", "sp"), "tp"),
            P(("grp", "sp"), "tp"),
            P(("grp", "sp"), "tp"),
            P("grp", None),
            P("tp", "sp"),
            P("grp", None, ("tp", "sp")),
            P("grp", None, ("sp", "tp")),
            P(),
            P(),
        ),
        out_specs=P(("grp", "tp"), "sp"),
        check_vma=False,
    )
```

```python
import functools

import jax
import jax.numpy as jnp
from jax import lax
from jax.experimental import pallas as pl
from jax.experimental.pallas import tpu as pltpu
from jax.sharding import PartitionSpec as P

HS = 128
RANK = 64
BLOCK = 128
BLOCKS = 5
NSP = 4
NTP = 8
NCHIP = 4
NZ = 8
SLOTS = 4
HEADS = 8
ROWS = 160
HALF = 80
FEAT = 1024
COLS = 2048
SLICE = 256
PARTS = 4
PCOLS = COLS // PARTS
TILE = 256
STACK = 8
PIECES = ((0, 16), (16, 64))

adapter_scale = 0.5
big_negative = -1e30
MESH = pl.DeviceIdType.MESH
F32 = jnp.float32
BF16 = jnp.bfloat16


def copy_to(src, dst, ssem, rsem, **axis):
    return pltpu.make_async_remote_copy(
        src_ref=src, dst_ref=dst, send_sem=ssem, recv_sem=rsem, device_id=axis, device_id_type=MESH
    )


def kernel(
    tas, tpb, plen, q_hbm, k_hbm, v_hbm, w_hbm, dn_hbm, up_hbm, out_ref,
    qv, kv, vv, wv, dnv, upv, probs, att, keep, sibs, sibr, xs, xr, hop, fin,
    zs, zr0, zr1, cross, crossr, down, up2own, up2, lxs, lxr, lrs, lyx, lrr,
    lsem, kvs, kvr, atts, attr, zss, zrs, crs, crr, ups, upr,
    sbs, sbr, xss, xrs, txs, txr, lxss, lxrs, lys, lyr, z_in,
):
    sp = lax.axis_index("sp")
    tp = lax.axis_index("tp")
    grp = lax.axis_index("grp")
    chip = tp // 2
    core = tp % 2
    sib = tp + 1 - 2 * core
    y_lo = grp // NZ
    z = grp % NZ
    other = (1 - y_lo) * NZ + z
    zr = (zr0, zr1)
    right = (sp + 1) % NSP
    left = (sp + NSP - 1) % NSP

    loads = [
        pltpu.make_async_copy(k_hbm, kv.at[2], lsem.at[0]),
        pltpu.make_async_copy(q_hbm, qv, lsem.at[1]),
        pltpu.make_async_copy(v_hbm, vv.at[2], lsem.at[2]),
        pltpu.make_async_copy(dn_hbm, dnv, lsem.at[3]),
        pltpu.make_async_copy(up_hbm, upv, lsem.at[4]),
        pltpu.make_async_copy(w_hbm, wv, lsem.at[5]),
    ]
    barrier = pltpu.get_barrier_semaphore()
    for i in range(1, NSP):
        pl.semaphore_signal(barrier, inc=1, device_id={"sp": (sp + i) % NSP}, device_id_type=MESH)
    for i in range(1, NTP):
        pl.semaphore_signal(barrier, inc=1, device_id={"tp": (tp + i) % NTP}, device_id_type=MESH)
    pl.semaphore_signal(barrier, inc=1, device_id={"grp": other}, device_id_type=MESH)
    for i in range(1, NZ):
        @pl.when(z + i < NZ)
        def _():
            pl.semaphore_signal(barrier, inc=1, device_id={"grp": grp + i}, device_id_type=MESH)

    for c in loads:
        c.start()
    pl.semaphore_wait(barrier, (NSP - 1) + (NTP - 1) + 1 + z)
    for i in range(1, NZ):
        @pl.when(z >= i)
        def _():
            pl.semaphore_signal(z_in, inc=1, device_id={"grp": grp - i}, device_id_type=MESH)


    def kv_copy(m, i):
        return copy_to(
            (k_hbm, v_hbm)[m], (kv, vv)[m].at[2 - i], kvs.at[m, i - 1], kvr.at[m, i - 1],
            sp=(sp + i) % NSP,
        )

    for m in range(2):
        for i in (1, 2):
            @pl.when(sp + i < NSP)
            def _():
                kv_copy(m, i).start()

    loads[3].wait()
    loads[4].wait()

    def slot_of(g, b):
        return tas[tpb[b, g]]

    def pack(g, carry):
        pick = jnp.int32(0)
        for b in range(BLOCKS):
            slot = slot_of(g, b)
            pick = pick + jnp.where(slot // SLOTS == grp, slot % SLOTS, 0)
        zs[0, g % NZ, g // NZ] = dnv[pick]
        zs[1, g % NZ, g // NZ] = upv[pick]
        return carry

    lax.fori_loop(0, 2 * NZ, pack, 0)

    def z_copy(m, i):
        to = (z + i) % NZ
        return copy_to(
            zs.at[m, to], zr[m].at[z], zss.at[m, i - 1], zrs.at[m, i - 1], grp=y_lo * NZ + to
        )

    for m in (1, 0):
        for i in range(1, NZ):
            @pl.when(z + i >= NZ)
            def _():
                z_copy(m, i).start()

    for m in range(2):
        for j in range(2):
            zr[m][z, j] = zs[m, z, j]

    def kv_ready(m):
        for i in (1, 2):
            @pl.when(sp >= i)
            def _():
                kv_copy(m, i).wait_recv()

            @pl.when(sp < i)
            def _():
                (kv, vv)[m][2 - i] = jnp.zeros((ROWS, HS), BF16)

    loads[0].wait()
    loads[1].wait()
    kv_ready(0)
    end0 = plen[0, 0]
    end1 = end0 + plen[0, 1]
    keys = kv[...].reshape(3 * ROWS, HS)
    for h in range(2):
        qpos = sp * ROWS + h * HALF + lax.broadcasted_iota(jnp.int32, (HALF, 3 * ROWS), 0)
        kpos = (sp - 2) * ROWS + lax.broadcasted_iota(jnp.int32, (HALF, 3 * ROWS), 1)
        first = jnp.where(qpos >= end1, end1, jnp.where(qpos >= end0, end0, 0))
        allowed = (kpos <= qpos) & (kpos >= first)
        for n in range(0, HEADS, STACK):
            qh = jnp.concatenate(
                [qv[h * HALF:(h + 1) * HALF, m * HS:(m + 1) * HS] for m in range(n, n + STACK)], axis=0
            )
            s = lax.dot_general(qh, keys, (((1,), (1,)), ((), ())), preferred_element_type=F32)
            s = jnp.where(
                allowed[None], s.reshape(STACK, HALF, 3 * ROWS) * HS ** -0.5, big_negative
            )
            p = jnp.exp(s - jnp.max(s, axis=2, keepdims=True))
            probs[h, n * HALF:(n + STACK) * HALF] = p.astype(BF16).reshape(STACK * HALF, 3 * ROWS)
    loads[2].wait()
    kv_ready(1)
    vals = jnp.concatenate(
        [vv[...].reshape(3 * ROWS, HS), jnp.ones((3 * ROWS, HS), BF16)], axis=1
    )

    def first_copy(side):
        return copy_to(
            att.at[0, side], att.at[1, side], atts.at[side, 0], attr.at[side, 0],
            sp=(right, left)[side],
        )

    def later_copy(side, piece):
        rows = pl.ds(*PIECES[piece])
        return copy_to(
            att.at[0, 1 - side, rows], att.at[3, 1 - side, rows],
            atts.at[side, 1 + piece], attr.at[side, 1 + piece],
            sp=(right, left)[side],
        )

    def relay(side):
        return copy_to(
            att.at[1, side], att.at[2, side], atts.at[side, 3], attr.at[side, 3],
            sp=(right, left)[side],
        )

    for h in range(2):
        for n in range(0, HEADS, STACK):
            o = jnp.dot(
                probs[h, n * HALF:(n + STACK) * HALF], vals, preferred_element_type=F32
            )
            o = (o[:, :HS] / o[:, HS:]).astype(BF16)
            for m in range(STACK):
                att[0, h, :, (n + m) * HS:(n + m + 1) * HS] = o[m * HALF:(m + 1) * HALF]
        first_copy(h).start()
    for side in range(2):
        later_copy(side, 0).start()

    @pl.when(z < NZ - 1)
    def _():
        pl.semaphore_wait(z_in, NZ - 1 - z)

    for m in (1, 0):
        for i in range(1, NZ):
            @pl.when(z + i < NZ)
            def _():
                z_copy(m, i).start()

    loads[5].wait()

    shift = 2 * core - 1
    keep_block = [sp, (sp + NSP + shift) % NSP, (sp + 2) % NSP, (sp + NSP - shift) % NSP]

    def sib_copy(k, part):
        cols = pl.ds(part * PCOLS, PCOLS)
        return copy_to(sibs.at[k, :, cols], sibr.at[k, :, cols], sbs.at[k, part], sbr.at[k, part], tp=sib)

    def product_part(k, part):
        for n in range(PCOLS // TILE):
            cols = pl.ds(part * PCOLS + n * TILE, TILE)
            v = jnp.dot(
                att[k].reshape(ROWS, FEAT), wv[:, cols], preferred_element_type=F32
            )
            keep[k, :, cols] = jnp.where(core == 0, v[:HALF], v[HALF:])
            sibs[k, :, cols] = jnp.where(core == 0, v[HALF:], v[:HALF]).astype(BF16)
        sib_copy(k, part).start()

    def product(k):
        for part in range(PARTS):
            product_part(k, part)

    def x_copy(k, part):
        cols = pl.ds(part * PCOLS, PCOLS)
        rel = (chip + NCHIP - keep_block[k] + NCHIP - 1) % NCHIP
        return copy_to(
            xs.at[k, :, cols], xr.at[rel, :, cols], xss.at[k, part], xrs.at[rel, part],
            tp=2 * keep_block[k] + core,
        )

    def x_part(k, part):
        cols = pl.ds(part * PCOLS, PCOLS)
        sib_copy(k, part).wait_recv()
        total = keep[k, :, cols] + sibr[k, :, cols].astype(F32)

        @pl.when(keep_block[k] == chip)
        def _():
            fin[:, cols] = total

        @pl.when(keep_block[k] != chip)
        def _():
            xs[k, :, cols] = total.astype(BF16)
            x_copy(k, part).start()

    def x_phase(k):
        for part in range(PARTS):
            x_part(k, part)

    far = (sp + 2) % NSP
    place = (chip + NCHIP - far) % NCHIP

    def tree_copy(part):
        cols = pl.ds(part * PCOLS, PCOLS)
        side = part // (PARTS // 2)
        to = (far + (1, NCHIP - 1)[side]) % NCHIP
        return copy_to(
            xs.at[2, :, cols], hop.at[part % (PARTS // 2)], txs.at[part], txr.at[part % (PARTS // 2)],
            tp=2 * to + core,
        )

    def far_phase():
        k = 2
        for part in range(PARTS):
            cols = pl.ds(part * PCOLS, PCOLS)
            side = part // (PARTS // 2)
            sib_copy(k, part).wait_recv()
            total = keep[k, :, cols] + sibr[k, :, cols].astype(F32)

            @pl.when(place == 0)
            def _():
                fin[:, cols] = total

            @pl.when(place == 2)
            def _():
                xs[k, :, cols] = total.astype(BF16)
                tree_copy(part).start()

            @pl.when(place == (3, 1)[side])
            def _():
                xs[k, :, cols] = total.astype(BF16)
                x_copy(k, part).start()

            @pl.when(place == (1, 3)[side])
            def _():
                keep[k, :, cols] = total

        for part in range(PARTS):
            cols = pl.ds(part * PCOLS, PCOLS)
            side = part // (PARTS // 2)

            @pl.when(place == (1, 3)[side])
            def _():
                tree_copy(part).wait_recv()
                total = keep[k, :, cols] + hop[part % (PARTS // 2)].astype(F32)
                xs[k, :, cols] = total.astype(BF16)
                x_copy(k, part).start()

        @pl.when(place == 0)
        def _():
            xr[1] = jnp.zeros((HALF, COLS), BF16)

    lane = lax.broadcasted_iota(jnp.int32, (HALF, 2 * RANK), 1)
    row = lax.broadcasted_iota(jnp.int32, (HALF, 2 * RANK), 0)
    features = pl.ds(pl.multiple_of(sp * SLICE, SLICE), SLICE)
    blocks_of = [(sp, sp), (left, right), (far, far), (right, left)]

    def low_copy(k, h):
        to = 2 * blocks_of[k][h] + h
        rel = (tp + NTP - to + NTP - 1) % NTP
        return copy_to(lxs.at[k, h], lxr.at[rel], lxss.at[k, h], lxrs.at[rel], tp=to)

    def low_rank(k):
        for h in range(2):
            sb = blocks_of[k][h]
            pair = down[pl.ds(sb, 2)].reshape(2 * RANK, SLICE)
            lr = lax.dot_general(
                att[k, h, :, features], pair, (((1,), (1,)), ((), ())), preferred_element_type=F32
            )
            early = (row + h * HALF < BLOCK - (ROWS - BLOCK) * sb).astype(jnp.int32)
            firsts = (lane < RANK).astype(jnp.int32)
            lr = jnp.where(early == firsts, lr, 0.0)

            @pl.when(2 * sb + h == tp)
            def _():
                lrs[...] = lr

            @pl.when(2 * sb + h != tp)
            def _():
                lxs[k, h] = lr.astype(BF16)
                low_copy(k, h).start()

    def cross_copy(m):
        return copy_to(cross.at[m], crossr.at[m], crs.at[m], crr.at[m], grp=other)

    def cross_send(m):
        for i in range(1, NZ):
            z_copy(m, i).wait_recv()

        def fill(b, carry):
            owner = slot_of(other, b) // SLOTS
            cross[m, b] = zr[m][owner % NZ, 1 - y_lo]
            return carry

        lax.fori_loop(0, BLOCKS, fill, 0)
        cross_copy(m).start()

    def cross_take(m, dst):
        cross_copy(m).wait_recv()

        def fill(b, carry):
            owner = slot_of(grp, b) // SLOTS
            dst[b] = jnp.where(owner // NZ == y_lo, zr[m][owner % NZ, y_lo], crossr[m, b])
            return carry

        lax.fori_loop(0, BLOCKS, fill, 0)

    def up_copy(i):
        to = (chip + i) % NCHIP
        return copy_to(
            up2own.at[pl.ds(to, 2)], up2.at[tp], ups.at[i - 1], upr.at[i - 1], tp=2 * to + core
        )

    def up_share(i):
        at = 2 * ((chip + NCHIP - i) % NCHIP) + core
        return copy_to(
            up2.at[at], up2.at[at], ups.at[NCHIP - 1 + i], upr.at[NCHIP - 1 + i], tp=sib
        )

    product(0)

    for side in range(2):
        first_copy(side).wait_recv()
        relay(side).start()
    for side in range(2):
        later_copy(side, 1).start()
    x_phase(0)
    product(1)
    x_phase(1)
    cross_send(0)

    for side in range(2):
        relay(side).wait_recv()
    product(2)
    far_phase()
    cross_take(0, down)
    for k in range(3):
        low_rank(k)
    cross_send(1)

    for side in range(2):
        for piece in range(2):
            later_copy(side, piece).wait_recv()
    low_rank(3)
    for part in range(PARTS):
        product_part(3, part)
        if part > 0:
            x_part(3, part - 1)
    x_part(3, PARTS - 1)
    cross_take(1, up2own)
    for i in range(1, NCHIP):
        up_copy(i).start()
    up2[tp] = up2own[pl.ds(chip, 2)]
    up_share(0).start()

    for rel in range(NTP - 1):
        copy_to(lxs.at[0, 0], lxr.at[rel], lxss.at[0, 0], lxrs.at[rel], tp=sib).wait_recv()
    low = lrs[...]
    for rel in range(NTP - 1):
        low = low + lxr[rel].astype(F32)
    lrs[...] = low
    lyx[...] = low.astype(BF16)

    def ly_copy(i):
        return copy_to(lyx, lrr.at[i - 1], lys.at[i - 1], lyr.at[i - 1], sp=(sp + i) % NSP)

    for i in range(1, NSP):
        ly_copy(i).start()

    for i in range(1, NCHIP):
        up_copy(i).wait_recv()
        up_share(i).start()
    for i in range(1, NSP):
        ly_copy(i).wait_recv()
    low = lrs[...]
    for i in range(NSP - 1):
        low = low + lrr[i].astype(F32)
    low = low.astype(BF16)
    for i in range(NCHIP):
        up_share(i).wait_recv()
    for part in range(PARTS):
        cols = pl.ds(part * PCOLS, PCOLS)
        for rel in range(NCHIP - 1):
            came = copy_to(
                xs.at[0, :, cols], xr.at[rel, :, cols], xss.at[0, part], xrs.at[rel, part], tp=sib
            )
            if rel == 1:
                @pl.when(place != 0)
                def _():
                    came.wait_recv()
            else:
                came.wait_recv()
        for n in range(PCOLS // SLICE):
            j = part * (PCOLS // SLICE) + n
            c = pl.ds(j * SLICE, SLICE)
            delta = jnp.dot(low, up2[j].reshape(2 * RANK, SLICE), preferred_element_type=F32)
            base = fin[:, c] + (
                xr[0, :, c].astype(F32) + xr[1, :, c].astype(F32) + xr[2, :, c].astype(F32)
            )
            out_ref[:, c] = (base + adapter_scale * delta).astype(BF16)

    for m in range(2):
        for i in (1, 2):
            @pl.when(sp + i < NSP)
            def _():
                kv_copy(m, i).wait_send()
        for i in range(1, NZ):
            z_copy(m, i).wait_send()
        cross_copy(m).wait_send()
    for side in range(2):
        first_copy(side).wait_send()
        relay(side).wait_send()
        for piece in range(2):
            later_copy(side, piece).wait_send()
    for i in range(1, NCHIP):
        up_copy(i).wait_send()
    for i in range(NCHIP):
        up_share(i).wait_send()
    for k in range(4):
        for part in range(PARTS):
            sib_copy(k, part).wait_send()

        if k == 2:
            @pl.when(place == 2)
            def _():
                for part in range(PARTS):
                    tree_copy(part).wait_send()

            @pl.when(place % 2 == 1)
            def _():
                for part in range(PARTS):
                    x_copy(k, part).wait_send()
        else:
            @pl.when(keep_block[k] != chip)
            def _():
                for part in range(PARTS):
                    x_copy(k, part).wait_send()

        for h in range(2):
            @pl.when(2 * blocks_of[k][h] + h != tp)
            def _():
                low_copy(k, h).wait_send()
    for i in range(1, NSP):
        ly_copy(i).wait_send()


def on_device(q, k, v, plen, w, dn, up, tas, tpb):
    smem = pl.BlockSpec(memory_space=pltpu.SMEM)
    anym = pl.BlockSpec(memory_space=pl.ANY)
    V = pltpu.VMEM
    D = pltpu.SemaphoreType.DMA
    return pl.pallas_call(
        kernel,
        out_shape=jax.ShapeDtypeStruct((HALF, COLS), BF16),
        in_specs=[smem] * 3 + [anym] * 6,
        out_specs=pl.BlockSpec(memory_space=pltpu.VMEM),
        scratch_shapes=[
            V((ROWS, FEAT), BF16),
            V((3, ROWS, HS), BF16),
            V((3, ROWS, HS), BF16),
            V((FEAT, COLS), BF16),
            V((SLOTS, RANK, SLICE), BF16),
            V((SLOTS, RANK, SLICE), BF16),
            V((2, HEADS * HALF, 3 * ROWS), BF16),
            V((4, 2, HALF, FEAT), BF16),
            V((4, HALF, COLS), F32),
            V((4, HALF, COLS), BF16),
            V((4, HALF, COLS), BF16),
            V((4, HALF, COLS), BF16),
            V((NCHIP - 1, HALF, COLS), BF16),
            V((PARTS // 2, HALF, PCOLS), BF16),
            V((HALF, COLS), F32),
            V((2, NZ, 2, RANK, SLICE), BF16),
            V((NZ, 2, RANK, SLICE), BF16),
            V((NZ, 2, RANK, SLICE), BF16),
            V((2, BLOCKS, RANK, SLICE), BF16),
            V((2, BLOCKS, RANK, SLICE), BF16),
            V((BLOCKS, RANK, SLICE), BF16),
            V((BLOCKS, RANK, SLICE), BF16),
            V((NTP, 2, RANK, SLICE), BF16),
            V((4, 2, HALF, 2 * RANK), BF16),
            V((NTP - 1, HALF, 2 * RANK), BF16),
            V((HALF, 2 * RANK), F32),
            V((HALF, 2 * RANK), BF16),
            V((NSP - 1, HALF, 2 * RANK), BF16),
            D((6,)),
            D((2, 2)), D((2, 2)),
            D((2, 4)), D((2, 4)),
            D((2, NZ - 1)), D((2, NZ - 1)),
            D((2,)), D((2,)),
            D((2 * NCHIP - 1,)), D((2 * NCHIP - 1,)),
            D((4, PARTS)), D((4, PARTS)),
            D((4, PARTS)), D((NCHIP - 1, PARTS)),
            D((PARTS,)), D((PARTS // 2,)),
            D((4, 2)), D((NTP - 1,)),
            D((NSP - 1,)), D((NSP - 1,)),
            pltpu.SemaphoreType.REGULAR,
        ],
        compiler_params=pltpu.CompilerParams(
            collective_id=0, has_side_effects=True, vmem_limit_bytes=56 * 1024 * 1024
        ),
    )(tas, tpb.T, plen, q, k, v, w, dn, up)


def solution(mesh):
    return jax.shard_map(
        on_device,
        mesh=mesh,
        in_specs=(
            P(("grp", "sp"), "tp"),
            P(("grp", "sp"), "tp"),
            P(("grp", "sp"), "tp"),
            P("grp", None),
            P("tp", "sp"),
            P("grp", None, ("tp", "sp")),
            P("grp", None, ("sp", "tp")),
            P(),
            P(),
        ),
        out_specs=P(("grp", "tp"), "sp"),
        check_vma=False,
    )
```
